32 devices in a mesh: line: 8 (over z, core), scan: 4 (over y, x).
Axes of the slice: x: 2, y: 2, z: 4, core: 2. Of those that a mesh axis runs over, the one named last changes fastest.
Arguments:
- query_row: bfloat16 [8, 512, 512], P('line', 'scan'), may hold values from -6 to 6
- key_row: bfloat16 [8, 512, 512], P('line', 'scan'), may hold values from -6 to 6
- value_row: bfloat16 [8, 512, 512], P('line', 'scan'), may hold values from -6 to 6
- decay_row: float32 [8, 512, 4], P('line', 'scan'), may hold values from -2 to 0
- beta_row: float32 [8, 512, 4], P('line', 'scan'), may hold values from 0.02 to 0.2
- gain_row: float32 [128], replicated, may hold values from 0.1 to 1.9
- query_col: bfloat16 [8, 4, 128, 512], P(None, 'scan', 'line'), may hold values from -6 to 6
- key_col: bfloat16 [8, 4, 128, 512], P(None, 'scan', 'line'), may hold values from -6 to 6
- decay_col: float32 [8, 4, 128, 4], P(None, 'scan', 'line'), may hold values from -2 to 0
- beta_col: float32 [8, 4, 128, 4], P(None, 'scan', 'line'), may hold values from 0.02 to 0.2
- gain_col: float32 [128], replicated, may hold values from 0.1 to 1.9
Outputs:
- mixed: bfloat16 [8, 512, 512], P('line', 'scan')
The draws below stay inside these ranges and needn't reach their ends.
All inputs are finite; a program needn't handle non-finite values.
Results may differ from the reference program's by a relative error of at most 0.0049.
Values may be sent and summed in bfloat16 or wider, within the bound.
A program may use at most 64 MiB of HBM per device.

```python
import math
import jax
import jax.numpy as jnp
from jax import lax

SEG = 128
HEAD_GROUP = 4
DK = 128
F = 512
H = 8
SEGS = 4
W = 512
CB = 8


def decay_field(key, leading_count, sequence_length):
    random_subkeys = jax.random.split(key, 6)
    slow_share = 0.5
    choose = jax.random.uniform(random_subkeys[0], (HEAD_GROUP,))
    slow_rate = jnp.exp(jax.random.uniform(random_subkeys[1], (HEAD_GROUP,), minval=-1.6, maxval=0.0)) / sequence_length
    fast_scale = 30.0 * jnp.exp(jax.random.uniform(random_subkeys[2], (HEAD_GROUP,), minval=0.0, maxval=2.302585))
    fast_rate = 1.0 / fast_scale
    baseline_rate = jnp.where(choose < slow_share, slow_rate, fast_rate)
    block_extent = min(SEG, sequence_length)
    number_of_blocks = sequence_length // block_extent
    token_multiplier = jnp.exp(jax.random.uniform(random_subkeys[3], (leading_count, number_of_blocks, block_extent, HEAD_GROUP), minval=-0.7, maxval=0.7))
    block_multiplier = jnp.exp(jax.random.uniform(random_subkeys[4], (leading_count, number_of_blocks, 1, HEAD_GROUP), minval=-0.7, maxval=0.7))
    spike_sample = jax.random.uniform(random_subkeys[5], (2, leading_count, number_of_blocks, block_extent, HEAD_GROUP))
    spike_events = jnp.where(spike_sample[0] < 2.0 / sequence_length, jnp.log(0.5 + 0.3 * spike_sample[1]), 0.0)
    token_grid = -baseline_rate * token_multiplier * block_multiplier + spike_events
    return token_grid.reshape(leading_count, sequence_length, HEAD_GROUP).astype(jnp.float32)


def drawn_keys(key, leading_count, sequence_length):
    random_subkeys = jax.random.split(key, 2)
    shared = jax.random.normal(random_subkeys[0], (leading_count, 1, HEAD_GROUP, DK), dtype=jnp.float32)
    shared_weight = 0.8944272
    noise_weight = 0.4472136
    noise = jax.random.normal(random_subkeys[1], (leading_count, sequence_length, HEAD_GROUP, DK), dtype=jnp.float32)
    field = jnp.clip(shared_weight * shared + noise_weight * noise, -6.0, 6.0)
    return field.reshape(leading_count, sequence_length, HEAD_GROUP * DK).astype(jnp.float32)


def draw_key_row(key, part):
    return drawn_keys(jax.random.fold_in(key, 31), H, W).astype(jnp.bfloat16)


def draw_key_col(key, part):
    field = drawn_keys(jax.random.fold_in(key, 37), W, H)
    return field.transpose(1, 0, 2).reshape(H, SEGS, SEG, HEAD_GROUP * DK).astype(jnp.bfloat16)


def draw_decay_row(key, part):
    return decay_field(jax.random.fold_in(key, 11), H, W)


def draw_decay_col(key, part):
    token_grid = decay_field(jax.random.fold_in(key, 23), W, H)
    return token_grid.transpose(1, 0, 2).reshape(H, SEGS, SEG, HEAD_GROUP)


def block_levels(key, shape, cuts, smallest, top_value):
    loudness, own = 1.0, jax.random.fold_in(key, 6)
    for dim, blocks in cuts:
        draws = jnp.exp(jax.random.uniform(jax.random.fold_in(own, dim), (blocks,), jnp.float32, smallest / len(cuts), top_value / len(cuts)))
        loudness = loudness * jnp.repeat(draws, shape[dim] // blocks).reshape([-1 if axis == dim else 1 for axis in range(len(shape))])
    return loudness


def gaussian(stream_key, dims, deviation, reach, cuts=(), held_as=jnp.bfloat16):
    loudness = block_levels(stream_key, dims, cuts, -0.22, 0.18) if cuts else 1.0
    result = jax.random.normal(stream_key, dims, jnp.float32) * deviation * loudness
    return jnp.minimum(jnp.maximum(result, -reach), reach).astype(held_as)


def setup_inputs(seed: int = 0) -> dict:
    seeds = jax.random.split(jax.random.key(seed), 12)
    query_row = gaussian(seeds[0], (H, W, F), 1.0, 6.0, ((0, 8), (1, 4)))
    key_row = draw_key_row(jax.random.fold_in(seeds[11], 71), 0)
    value_row = gaussian(seeds[2], (H, W, F), 1.0, 6.0, ((0, 8), (1, 4)))
    decay_row = draw_decay_row(jax.random.fold_in(seeds[11], 71), 0)
    beta_row = jnp.clip(jnp.exp(math.log(0.2) - 2.3025851 * jax.random.uniform(seeds[4], (H, W, HEAD_GROUP), jnp.float32) ** block_levels(seeds[4], (H, W, HEAD_GROUP), ((0, 8), (1, 4)), -0.2, 0.2)), 0.02, 0.2)
    gain_row = jnp.clip(1.0 + 0.18 * jax.random.normal(seeds[5], (DK,), jnp.float32), 0.1, 1.9)
    query_col = gaussian(seeds[6], (H, SEGS, SEG, F), 1.0, 6.0, ((1, 4), (2, 8)))
    key_col = draw_key_col(jax.random.fold_in(seeds[11], 71), 0)
    decay_col = draw_decay_col(jax.random.fold_in(seeds[11], 71), 0)
    beta_col = jnp.clip(jnp.exp(math.log(0.2) - 2.3025851 * jax.random.uniform(seeds[9], (H, SEGS, SEG, HEAD_GROUP), jnp.float32) ** block_levels(seeds[9], (H, SEGS, SEG, HEAD_GROUP), ((1, 4), (2, 8)), -0.2, 0.2)), 0.02, 0.2)
    gain_col = jnp.clip(1.0 + 0.18 * jax.random.normal(seeds[10], (DK,), jnp.float32), 0.1, 1.9)
    return {"query_row": query_row, "key_row": key_row, "value_row": value_row, "decay_row": decay_row, "beta_row": beta_row, "gain_row": gain_row, "query_col": query_col, "key_col": key_col, "decay_col": decay_col, "beta_col": beta_col, "gain_col": gain_col}


HIGHEST = lax.Precision.HIGHEST

def block_terms(query_block, key_block, value_block, log_decay, beta_block):
    key_unit = key_block / jnp.sqrt(lax.optimization_barrier(jnp.sum(key_block * key_block, axis=-1, keepdims=True)) + 1e-06)
    cumulative = jnp.cumsum(log_decay, axis=-1)
    sequence_length = key_block.shape[1]
    lower_mask = jnp.tril(jnp.ones((sequence_length, sequence_length), dtype=jnp.bool_))
    strict = jnp.tril(jnp.ones((sequence_length, sequence_length), dtype=jnp.bool_), -1)
    spread = cumulative[:, :, None] - cumulative[:, None, :]
    ratios = jnp.where(lower_mask, jnp.exp(jnp.where(lower_mask, spread, 0.0)), 0.0)
    key_inner = jnp.einsum('bik,bjk->bij', key_unit, key_unit, precision=HIGHEST)
    system = jnp.where(strict, beta_block[:, :, None] * ratios * key_inner, 0.0) + jnp.eye(sequence_length, dtype=jnp.float32)
    growth = jnp.exp(cumulative)
    right_side = jnp.concatenate([beta_block[:, :, None] * value_block, (beta_block * growth)[:, :, None] * key_unit], axis=-1)
    solved = jax.scipy.linalg.solve_triangular(system, right_side, lower=True)
    value_size = value_block.shape[-1]
    updates = solved[:, :, :value_size]
    weighted = solved[:, :, value_size:]
    attend = ratios * jnp.einsum('bik,bjk->bij', query_block, key_unit, precision=HIGHEST)
    local_out = jnp.einsum('bij,bjv->biv', attend, updates, precision=HIGHEST)
    state_query = growth[:, :, None] * query_block - jnp.einsum('bij,bjk->bik', attend, weighted, precision=HIGHEST)
    key_tail = jnp.exp(cumulative[:, -1:] - cumulative)[:, :, None] * key_unit
    return (local_out, state_query, key_tail, weighted, updates, growth[:, -1])

def scan_blocks(queries, key_rows, values, log_decay, beta_rows, block_extent):
    batch_size, sequence_length, head_size = queries.shape
    number_of_blocks = sequence_length // block_extent

    def blocks(array):
        return array.reshape((batch_size, number_of_blocks, block_extent) + array.shape[2:]).swapaxes(0, 1)

    def advance(carried, pieces):
        local_out, state_query, key_tail, weighted, updates, ending = block_terms(*pieces)
        output = local_out + jnp.einsum('bik,bkv->biv', state_query, carried, precision=HIGHEST)
        residue = updates - jnp.einsum('bjk,bkv->bjv', weighted, carried, precision=HIGHEST)
        carried = ending[:, None, None] * carried + jnp.einsum('bjk,bjv->bkv', key_tail, residue, precision=HIGHEST)
        return (carried, output)
    initial = jnp.zeros((batch_size, head_size, head_size), dtype=jnp.float32)
    last_state, outputs = lax.scan(advance, initial, (blocks(queries), blocks(key_rows), blocks(values), blocks(log_decay), blocks(beta_rows)))
    return outputs.swapaxes(0, 1).reshape(batch_size, sequence_length, head_size)

def to_heads(array, leading_count, sequence_length, head_count, head_size):
    shaped = array.astype(jnp.float32).reshape(leading_count, sequence_length, head_count, head_size)
    return shaped.transpose(0, 2, 1, 3).reshape(leading_count * head_count, sequence_length, head_size)

def gates_to_heads(array, leading_count, sequence_length, head_count):
    return array.reshape(leading_count, sequence_length, head_count).transpose(0, 2, 1).reshape(leading_count * head_count, sequence_length)

def from_heads(array, leading_count, sequence_length, head_count, head_size):
    return array.reshape(leading_count, head_count, sequence_length, head_size).transpose(0, 2, 1, 3)

def head_norm(array, gain):
    return array * lax.rsqrt(lax.optimization_barrier(jnp.mean(array * array, axis=-1, keepdims=True)) + 1e-05) * gain

def columns(array):
    return array.reshape(H, W, -1).transpose(1, 0, 2)

def reference(query_row, key_row, value_row, decay_row, beta_row, gain_row, query_col, key_col, decay_col, beta_col, gain_col):
    row_out = scan_blocks(to_heads(query_row, H, W, HEAD_GROUP, DK), to_heads(key_row, H, W, HEAD_GROUP, DK), to_heads(value_row, H, W, HEAD_GROUP, DK), gates_to_heads(decay_row, H, W, HEAD_GROUP), gates_to_heads(beta_row, H, W, HEAD_GROUP), SEG)
    row_scan = from_heads(row_out, H, W, HEAD_GROUP, DK)
    values_col = head_norm(row_scan, gain_row).reshape(H, W, F).astype(jnp.bfloat16)
    values_col = lax.optimization_barrier(values_col)
    col_out = scan_blocks(to_heads(columns(query_col), W, H, HEAD_GROUP, DK), to_heads(columns(key_col), W, H, HEAD_GROUP, DK), to_heads(values_col.transpose(1, 0, 2), W, H, HEAD_GROUP, DK), gates_to_heads(columns(decay_col), W, H, HEAD_GROUP), gates_to_heads(columns(beta_col), W, H, HEAD_GROUP), CB)
    col_scan = from_heads(col_out, W, H, HEAD_GROUP, DK)
    mixed = head_norm(col_scan, gain_col).reshape(W, H, F).transpose(1, 0, 2)
    return mixed.astype(jnp.bfloat16)
```

```python
import functools

import jax
import jax.numpy as jnp
from jax import lax
from jax.experimental import pallas as pl
from jax.experimental.pallas import tpu as pltpu
from jax.sharding import PartitionSpec as P

F32 = jnp.float32
BF16 = jnp.bfloat16


def dot(a, b):
    return jnp.dot(a, b, preferred_element_type=F32)


def dot_t(a, b):
    return lax.dot_general(a, b, (((1,), (1,)), ((), ())), preferred_element_type=F32)


def split(a):
    high = a.astype(BF16)
    return high, (a - high.astype(F32)).astype(BF16)


def dot_left(a, b):
    high, low = split(a)
    return dot(high, b) + dot(low, b)


def dot_right(a, b):
    high, low = split(b)
    return dot(a, high) + dot(a, low)


def dot_pairs(a, b):
    return dot(a[0], b[0]) + (dot(a[0], b[1]) + dot(a[1], b[0]))


def masks(size, stride):
    row = lax.broadcasted_iota(jnp.int32, (size, size), 0)
    col = lax.broadcasted_iota(jnp.int32, (size, size), 1)
    same = lax.rem(row, stride) == lax.rem(col, stride)
    return row, col, row == col, same & (row >= col), same & (row > col)


def to_row(column, diagonal):
    return jnp.sum(jnp.where(diagonal, column, 0.0), axis=0, keepdims=True)


def inverse(systems, row, col, diagonal, stride, steps):
    unit = jnp.where(diagonal, 1.0, 0.0)
    base = min(16, steps)
    near = (row // (base * stride)) == (col // (base * stride))
    power = [jnp.where(near, m, 0.0) for m in systems]
    total = [unit - m for m in power]
    reach = 2
    while reach < base:
        halves = [split(m) for m in power]
        power = [dot_pairs(m, m) for m in halves]
        total = [t + dot_pairs(split(t), split(m)) for t, m in zip(total, power)]
        reach *= 2
    size = base
    while size < steps:
        wide = size * 2 * stride
        link = ((row // wide) == (col // wide)) & (
            (row // (size * stride)) != (col // (size * stride))
        )
        halves = [split(t) for t in total]
        inner = [
            dot_pairs(split(jnp.where(link, m, 0.0)), t) for m, t in zip(systems, halves)
        ]
        total = [
            t - dot_pairs(h, split(i)) for t, h, i in zip(total, halves, inner)
        ]
        size *= 2
    return total


def prepare(queries, keys, decay, beta, stride):
    size = keys[0].shape[0]
    steps = size // stride
    row, col, diagonal, lower, strict = masks(size, stride)
    cumulative = jnp.dot(
        jnp.where(lower, 1.0, 0.0), decay, precision=lax.Precision.HIGHEST, preferred_element_type=F32
    )
    heads = range(len(keys))
    cums = [cumulative[:, h : h + 1] for h in heads]
    betas = [beta[:, h : h + 1] for h in heads]
    ratios, systems, attends, units = [], [], [], []
    for h in heads:
        gram = dot_t(keys[h], keys[h])
        squares = jnp.where(diagonal, gram, 0.0)
        unit_col = lax.rsqrt(jnp.sum(squares, axis=1, keepdims=True) + 1e-06)
        unit_row = lax.rsqrt(jnp.sum(squares, axis=0, keepdims=True) + 1e-06)
        spread = cums[h] - to_row(cums[h], diagonal)
        ratio = jnp.where(lower, jnp.exp(jnp.where(lower, spread, 0.0)), 0.0) * unit_row
        systems.append(jnp.where(strict, (betas[h] * unit_col) * (ratio * gram), 0.0))
        attends.append(ratio * dot_t(queries[h], keys[h]))
        units.append(unit_col)
    solved = inverse(systems, row, col, diagonal, stride, steps)
    return solved, attends, cums, betas, units, diagonal


def normed(block, gain):
    return block * lax.rsqrt(jnp.mean(block * block, axis=-1, keepdims=True) + 1e-05) * gain


def each(count, body):
    if count <= 8:
        for i in range(count):
            body(i)
    else:
        lax.fori_loop(0, count, lambda i, c: (body(i), c)[1], 0)


def kernel(
    lines,
    scans,
    query_row,
    key_row,
    value_row,
    decay_row,
    beta_row,
    gain_row,
    query_col,
    key_col,
    decay_col,
    beta_col,
    gain_col,
    out,
    arrived,
    leaving,
    transfer,
    offset,
    local,
    asking,
    mixer,
    outgoing,
    incoming,
    returning,
    returned,
    state_send,
    state_recv,
    there_send,
    there_recv,
    back_send,
    back_recv,
):
    me = lax.axis_index("line")
    place = lax.axis_index("scan")
    tokens, features = query_row.shape[1:]
    size = gain_row.shape[1]
    heads = range(features // size)
    total_rows, width = query_col.shape[0], query_col.shape[2]

    barrier = pltpu.get_barrier_semaphore()

    def greet(i):
        pl.semaphore_signal(
            barrier, inc=1, device_id={"line": lax.rem(me + 1 + i, lines)},
            device_id_type=pl.DeviceIdType.MESH,
        )

    each(lines - 1, greet)

    @pl.when(place > 0)
    def _():
        pl.semaphore_signal(
            barrier, inc=1, device_id={"scan": place - 1}, device_id_type=pl.DeviceIdType.MESH
        )

    @pl.when(place < scans - 1)
    def _():
        pl.semaphore_signal(
            barrier, inc=1, device_id={"scan": place + 1}, device_id_type=pl.DeviceIdType.MESH
        )

    def of_head(ref, h):
        return ref[0, :, h * size : (h + 1) * size]

    queries = [of_head(query_row, h) for h in heads]
    keys = [of_head(key_row, h) for h in heads]
    solved, attends, cums, betas, units, diagonal = prepare(
        queries, keys, decay_row[0], beta_row[0], 1
    )
    for h in heads:
        growth = jnp.exp(cums[h])
        last = cums[h][tokens - 1 : tokens, :]
        tail = jnp.exp(last - cums[h]) * units[h]
        updates = dot_left(solved[h] * to_row(betas[h], diagonal), of_head(value_row, h))
        weighted = dot_left(
            solved[h] * to_row(betas[h] * growth * units[h], diagonal), keys[h]
        )
        both = jnp.concatenate([updates, weighted], axis=1)
        seen = dot_pairs(split(attends[h]), split(both))
        key_t = keys[h].astype(F32).T.astype(BF16)
        kept = dot_right(key_t, tail * both)
        offset[h] = kept[:, :size]
        transfer[h] = jnp.where(diagonal, jnp.exp(last), 0.0) - kept[:, size:]
        local[h] = seen[:, :size]
        asking[h] = growth * queries[h].astype(F32) - seen[:, size:]

    pl.semaphore_wait(
        barrier, lines - 1 + jnp.minimum(place, 1) + jnp.minimum(scans - 1 - place, 1)
    )

    def state_copy(h):
        return pltpu.make_async_remote_copy(
            src_ref=leaving.at[h],
            dst_ref=arrived.at[h],
            send_sem=state_send.at[h],
            recv_sem=state_recv.at[h],
            device_id={"scan": lax.rem(place + 1, scans)},
            device_id_type=pl.DeviceIdType.MESH,
        )

    @pl.when(place == 0)
    def _():
        for h in heads:
            leaving[h] = offset[h].astype(BF16)
            if scans > 1:
                state_copy(h).start()
            arrived[h] = jnp.zeros((size, size), BF16)

    def of_head_col(ref, h):
        block = ref[:, 0, :, h * size : (h + 1) * size]
        return block.reshape(total_rows * width, size)

    def column_terms():
        col_solved, col_attends, _, col_betas, _, col_diagonal = prepare(
            [of_head_col(query_col, h) for h in heads],
            [of_head_col(key_col, h) for h in heads],
            decay_col[:, 0].reshape(total_rows * width, -1),
            beta_col[:, 0].reshape(total_rows * width, -1),
            width,
        )
        for h in heads:
            mixer[h] = dot_pairs(
                split(col_attends[h]),
                split(col_solved[h] * to_row(col_betas[h], col_diagonal)),
            )

    column_terms()

    @pl.when(place > 0)
    def _():
        for h in heads:
            state_copy(h).wait_recv()

            @pl.when(place < scans - 1)
            def _():
                leaving[h] = (dot_left(transfer[h], arrived[h]) + offset[h]).astype(BF16)
                state_copy(h).start()

    def swap(source, target, send, recv, h, i, back=False):
        peer = lax.rem(me + 1 + i, lines)
        return pltpu.make_async_remote_copy(
            src_ref=source.at[h, peer],
            dst_ref=target.at[h, me],
            send_sem=send.at[h, i],
            recv_sem=recv.at[h, me],
            device_id={"line": peer},
            device_id_type=pl.DeviceIdType.MESH,
        )

    def receive(source, target, send, recv, h, i):
        peer = lax.rem(me + 1 + i, lines)
        pltpu.make_async_remote_copy(
            src_ref=source.at[h, peer],
            dst_ref=target.at[h, peer],
            send_sem=send.at[h, i],
            recv_sem=recv.at[h, peer],
            device_id={"line": peer},
            device_id_type=pl.DeviceIdType.MESH,
        ).wait_recv()

    there = (outgoing, incoming, there_send, there_recv)
    back = (returning, returned, back_send, back_recv)

    for h in heads:
        row_out = local[h] + dot_left(asking[h], arrived[h])
        values = normed(row_out, gain_row[...]).astype(BF16)
        outgoing[h] = values.reshape(lines, tokens // lines, size)
        each(lines - 1, lambda i: swap(*there, h, i).start())
        incoming[h, me] = outgoing[h, me]

    for h in heads:
        each(lines - 1, lambda i: receive(*there, h, i))
        values = incoming[h].reshape(total_rows * width, size)
        mixed = normed(dot_left(mixer[h], values), gain_col[...]).astype(BF16)
        returning[h] = mixed.reshape(total_rows, width, size)
        each(lines - 1, lambda i: swap(*back, h, i).start())
        returned[h, me] = returning[h, me]

    for h in heads:
        each(lines - 1, lambda i: receive(*back, h, i))
        out[0, :, h * size : (h + 1) * size] = returned[h].reshape(tokens, size)

    for h in heads:
        each(lines - 1, lambda i: swap(*there, h, i).wait_send())
        each(lines - 1, lambda i: swap(*back, h, i).wait_send())

    @pl.when(place < scans - 1)
    def _():
        for h in heads:
            state_copy(h).wait_send()


def shards(*arrays):
    query_row, gain_row, query_col = arrays[0], arrays[5], arrays[6]
    lines, scans = lax.axis_size("line"), lax.axis_size("scan")
    tokens, features = query_row.shape[1:]
    size = gain_row.shape[0]
    heads = features // size
    arrays = list(arrays)
    arrays[5] = arrays[5].reshape(1, size)
    arrays[10] = arrays[10].reshape(1, size)
    square = (heads, size, size)
    rows = (heads, tokens, size)
    swapped = (heads, lines, tokens // lines, size)
    vmem = pl.BlockSpec(memory_space=pltpu.VMEM)
    return pl.pallas_call(
        functools.partial(kernel, lines, scans),
        out_shape=jax.ShapeDtypeStruct(query_row.shape, BF16),
        in_specs=[vmem] * len(arrays),
        out_specs=vmem,
        scratch_shapes=[
            pltpu.VMEM(square, BF16),
            pltpu.VMEM(square, BF16),
            pltpu.VMEM(square, F32),
            pltpu.VMEM(square, F32),
            pltpu.VMEM(rows, F32),
            pltpu.VMEM(rows, F32),
            pltpu.VMEM(rows, F32),
            pltpu.VMEM(swapped, BF16),
            pltpu.VMEM(swapped, BF16),
            pltpu.VMEM(swapped, BF16),
            pltpu.VMEM(swapped, BF16),
            pltpu.SemaphoreType.DMA((heads,)),
            pltpu.SemaphoreType.DMA((heads,)),
            pltpu.SemaphoreType.DMA((heads, lines)),
            pltpu.SemaphoreType.DMA((heads, lines)),
            pltpu.SemaphoreType.DMA((heads, lines)),
            pltpu.SemaphoreType.DMA((heads, lines)),
        ],
        compiler_params=pltpu.CompilerParams(
            collective_id=0, has_side_effects=True, vmem_limit_bytes=32 * 1024 * 1024
        ),
    )(*arrays)


def solution(mesh):
    placed = (
        P("line", "scan", None),
        P("line", "scan", None),
        P("line", "scan", None),
        P("line", "scan", None),
        P("line", "scan", None),
        P(),
        P(None, "scan", "line", None),
        P(None, "scan", "line", None),
        P(None, "scan", "line", None),
        P(None, "scan", "line", None),
        P(),
    )
    return jax.shard_map(
        shards, mesh=mesh, in_specs=placed, out_specs=P("line", "scan", None), check_vma=False
    )
```

```python
import functools

import jax
import jax.numpy as jnp
from jax import lax
from jax.experimental import pallas as pl
from jax.experimental.pallas import tpu as pltpu
from jax.sharding import PartitionSpec as P

F32 = jnp.float32
BF16 = jnp.bfloat16


def dot(a, b):
    return jnp.dot(a, b, preferred_element_type=F32)


def dot_t(a, b):
    return lax.dot_general(a, b, (((1,), (1,)), ((), ())), preferred_element_type=F32)


def split(a):
    high = a.astype(BF16)
    return high, (a - high.astype(F32)).astype(BF16)


def dot_left(a, b):
    high, low = split(a)
    return dot(high, b) + dot(low, b)


def dot_right(a, b):
    high, low = split(b)
    return dot(a, high) + dot(a, low)


def dot_pairs(a, b):
    return dot(a[0], b[0]) + (dot(a[0], b[1]) + dot(a[1], b[0]))


def masks(size, stride):
    row = lax.broadcasted_iota(jnp.int32, (size, size), 0)
    col = lax.broadcasted_iota(jnp.int32, (size, size), 1)
    same = lax.rem(row, stride) == lax.rem(col, stride)
    return row, col, row == col, same & (row >= col), same & (row > col)


def to_row(column, diagonal):
    return jnp.sum(jnp.where(diagonal, column, 0.0), axis=0, keepdims=True)


def inverse(systems, row, col, diagonal, stride, steps):
    unit = jnp.where(diagonal, 1.0, 0.0)
    base = min(16, steps)
    near = (row // (base * stride)) == (col // (base * stride))
    power = [jnp.where(near, m, 0.0) for m in systems]
    total = [unit - m for m in power]
    reach = 2
    while reach < base:
        halves = [split(m) for m in power]
        power = [dot_pairs(m, m) for m in halves]
        total = [t + dot_pairs(split(t), split(m)) for t, m in zip(total, power)]
        reach *= 2
    size = base
    while size < steps:
        wide = size * 2 * stride
        link = ((row // wide) == (col // wide)) & (
            (row // (size * stride)) != (col // (size * stride))
        )
        halves = [split(t) for t in total]
        inner = [
            dot_pairs(split(jnp.where(link, m, 0.0)), t) for m, t in zip(systems, halves)
        ]
        total = [
            t - dot_pairs(h, split(i)) for t, h, i in zip(total, halves, inner)
        ]
        size *= 2
    return total


def prepare(queries, keys, decay, beta, stride):
    size = keys[0].shape[0]
    steps = size // stride
    row, col, diagonal, lower, strict = masks(size, stride)
    cumulative = jnp.dot(
        jnp.where(lower, 1.0, 0.0), decay, precision=lax.Precision.HIGHEST, preferred_element_type=F32
    )
    heads = range(len(keys))
    cums = [cumulative[:, h : h + 1] for h in heads]
    betas = [beta[:, h : h + 1] for h in heads]
    ratios, systems, attends, units = [], [], [], []
    for h in heads:
        gram = dot_t(keys[h], keys[h])
        squares = jnp.where(diagonal, gram, 0.0)
        unit_col = lax.rsqrt(jnp.sum(squares, axis=1, keepdims=True) + 1e-06)
        unit_row = lax.rsqrt(jnp.sum(squares, axis=0, keepdims=True) + 1e-06)
        spread = cums[h] - to_row(cums[h], diagonal)
        ratio = jnp.where(lower, jnp.exp(jnp.where(lower, spread, 0.0)), 0.0) * unit_row
        systems.append(jnp.where(strict, (betas[h] * unit_col) * (ratio * gram), 0.0))
        attends.append(ratio * dot_t(queries[h], keys[h]))
        units.append(unit_col)
    solved = inverse(systems, row, col, diagonal, stride, steps)
    return solved, attends, cums, betas, units, diagonal


def normed(block, gain):
    return block * lax.rsqrt(jnp.mean(block * block, axis=-1, keepdims=True) + 1e-05) * gain


def each(count, body):
    if count <= 8:
        for i in range(count):
            body(i)
    else:
        lax.fori_loop(0, count, lambda i, c: (body(i), c)[1], 0)


def kernel(
    lines,
    scans,
    *refs,
):
    hbm, out, held = refs[:11], refs[11], refs[12:23]
    (
        state,
        own,
        gift_out,
        gift_in,
        chain_out,
        chain_in,
        transfer,
        offset,
        local,
        asking,
        mixer,
        outgoing,
        incoming,
        returning,
        returned,
        load_sem,
        gift_send,
        gift_recv,
        chain_send,
        chain_recv,
        there_send,
        there_recv,
        back_send,
        back_recv,
    ) = refs[23:]
    (
        query_row,
        key_row,
        value_row,
        decay_row,
        beta_row,
        gain_row,
        query_col,
        key_col,
        decay_col,
        beta_col,
        gain_col,
    ) = held
    me = lax.axis_index("line")
    place = lax.axis_index("scan")
    odd = lax.rem(place, 2)
    tokens, features = query_row.shape[1:]
    size = gain_row.shape[1]
    heads = range(features // size)
    total_rows, width = query_col.shape[0], query_col.shape[2]
    groups = outgoing.shape[0]
    group_heads = outgoing.shape[2]
    mesh_id = pl.DeviceIdType.MESH

    def load(i):
        return pltpu.make_async_copy(hbm[i], held[i], load_sem.at[i])

    for i in (1, 3, 4, 0, 2, 5, 7, 6, 8, 9, 10):
        load(i).start()

    barrier = pltpu.get_barrier_semaphore()

    def greet(i):
        pl.semaphore_signal(
            barrier, inc=1, device_id={"line": lax.rem(me + 1 + i, lines)}, device_id_type=mesh_id
        )

    each(lines - 1, greet)

    def greet_along(distance):
        pl.semaphore_signal(
            barrier, inc=1, device_id={"scan": place + distance}, device_id_type=mesh_id
        )

    pl.when(place > 0)(lambda: greet_along(-1))
    pl.when(place < scans - 1)(lambda: greet_along(1))
    pl.when((odd == 1) & (place > 1))(lambda: greet_along(-2))
    pl.when((odd == 1) & (place < scans - 2))(lambda: greet_along(2))

    def of_head(ref, h):
        return ref[0, :, h * size : (h + 1) * size]

    for i in (1, 3, 4, 0):
        load(i).wait()
    queries = [of_head(query_row, h) for h in heads]
    keys = [of_head(key_row, h) for h in heads]
    solved, attends, cums, betas, units, diagonal = prepare(
        queries, keys, decay_row[0], beta_row[0], 1
    )
    load(2).wait()
    for h in heads:
        growth = jnp.exp(cums[h])
        last = cums[h][tokens - 1 : tokens, :]
        tail = jnp.exp(last - cums[h]) * units[h]
        updates = dot_left(solved[h] * to_row(betas[h], diagonal), of_head(value_row, h))
        weighted = dot_left(
            solved[h] * to_row(betas[h] * growth * units[h], diagonal), keys[h]
        )
        both = jnp.concatenate([updates, weighted], axis=1)
        own[h] = both
        key_t = keys[h].astype(F32).T.astype(BF16)
        kept = dot_right(key_t, tail * both)
        offset[h] = kept[:, :size]
        transfer[h] = jnp.where(diagonal, jnp.exp(last), 0.0) - kept[:, size:]

    pl.semaphore_wait(
        barrier,
        lines
        - 1
        + jnp.minimum(place, 1)
        + jnp.minimum(scans - 1 - place, 1)
        + odd * (jnp.minimum(place // 2, 1) + jnp.minimum((scans - 1 - place) // 2, 1)),
    )

    def gift(which, h):
        return pltpu.make_async_remote_copy(
            src_ref=gift_out.at[which, h],
            dst_ref=gift_in.at[which, h],
            send_sem=gift_send.at[which, h],
            recv_sem=gift_recv.at[which, h],
            device_id={"scan": lax.rem(place + 1, scans)},
            device_id_type=mesh_id,
        )

    def chain(h, distance):
        return pltpu.make_async_remote_copy(
            src_ref=chain_out.at[h],
            dst_ref=chain_in.at[h],
            send_sem=chain_send.at[distance - 1, h],
            recv_sem=chain_recv.at[h],
            device_id={"scan": lax.rem(place + distance, scans)},
            device_id_type=mesh_id,
        )

    gives = (odd == 0) & (place < scans - 1)

    @pl.when(gives)
    def _():
        for h in heads:
            gift_out[0, h] = offset[h].astype(BF16)
            gift(0, h).start()

            @pl.when(place > 0)
            def _():
                gift_out[1, h] = transfer[h].astype(BF16)
                gift(1, h).start()

    for h in heads:
        seen = dot_pairs(split(attends[h]), split(own[h]))
        local[h] = seen[:, :size]
        asking[h] = jnp.exp(cums[h]) * queries[h].astype(F32) - seen[:, size:]

    for i in (5, 7, 6, 8, 9, 10):
        load(i).wait()

    def of_head_col(ref, h):
        block = ref[:, 0, :, h * size : (h + 1) * size]
        return block.reshape(total_rows * width, size)

    def column_terms():
        col_solved, col_attends, _, col_betas, _, col_diagonal = prepare(
            [of_head_col(query_col, h) for h in heads],
            [of_head_col(key_col, h) for h in heads],
            decay_col[:, 0].reshape(total_rows * width, -1),
            beta_col[:, 0].reshape(total_rows * width, -1),
            width,
        )
        for h in heads:
            mixer[h] = dot_pairs(
                split(col_attends[h]),
                split(col_solved[h] * to_row(col_betas[h], col_diagonal)),
            )

    pl.when(place >= 2)(column_terms)

    @pl.when(place == 0)
    def _():
        state[...] = jnp.zeros_like(state)

    @pl.when(odd == 1)
    def _():
        for h in heads:
            gift(0, h).wait_recv()

            @pl.when(place == 1)
            def _():
                state[h] = gift_in[0, h]

            @pl.when(place > 1)
            def _():
                gift(1, h).wait_recv()
                chain(h, 1).wait_recv()
                state[h] = (
                    dot(gift_in[1, h], chain_in[h]) + gift_in[0, h].astype(F32)
                ).astype(BF16)

            @pl.when(place < scans - 1)
            def _():
                chain_out[h] = (dot_left(transfer[h], state[h]) + offset[h]).astype(BF16)
                chain(h, 1).start()
                pl.when(place < scans - 2)(lambda: chain(h, 2).start())

    @pl.when((odd == 0) & (place > 0))
    def _():
        for h in heads:
            chain(h, 1).wait_recv()
            state[h] = chain_in[h]

    def swap(source, target, send, recv, g, i):
        peer = lax.rem(me + 1 + i, lines)
        return pltpu.make_async_remote_copy(
            src_ref=source.at[g, peer],
            dst_ref=target.at[g, me],
            send_sem=send.at[g, i],
            recv_sem=recv.at[g, me],
            device_id={"line": peer},
            device_id_type=mesh_id,
        )

    def receive(source, target, send, recv, g, i):
        peer = lax.rem(me + 1 + i, lines)
        pltpu.make_async_remote_copy(
            src_ref=source.at[g, peer],
            dst_ref=target.at[g, peer],
            send_sem=send.at[g, i],
            recv_sem=recv.at[g, peer],
            device_id={"line": peer},
            device_id_type=mesh_id,
        ).wait_recv()

    there = (outgoing, incoming, there_send, there_recv)
    back = (returning, returned, back_send, back_recv)

    for g in range(groups):
        for j in range(group_heads):
            h = g * group_heads + j
            row_out = local[h] + dot_left(asking[h], state[h])
            values = normed(row_out, gain_row[...]).astype(BF16)
            outgoing[g, :, j] = values.reshape(lines, tokens // lines, size)
        each(lines - 1, lambda i: swap(*there, g, i).start())
        incoming[g, me] = outgoing[g, me]

    pl.when(place < 2)(column_terms)

    for g in range(groups):
        each(lines - 1, lambda i: receive(*there, g, i))
        for j in range(group_heads):
            h = g * group_heads + j
            values = incoming[g, :, j].reshape(total_rows * width, size)
            mixed = normed(dot_left(mixer[h], values), gain_col[...]).astype(BF16)
            returning[g, :, j] = mixed.reshape(total_rows, width, size)
        each(lines - 1, lambda i: swap(*back, g, i).start())
        returned[g, me] = returning[g, me]

    for g in range(groups):
        each(lines - 1, lambda i: receive(*back, g, i))
        for j in range(group_heads):
            h = g * group_heads + j
            out[0, :, h * size : (h + 1) * size] = returned[g, :, j].reshape(tokens, size)

    for g in range(groups):
        each(lines - 1, lambda i: swap(*there, g, i).wait_send())
        each(lines - 1, lambda i: swap(*back, g, i).wait_send())

    @pl.when(gives)
    def _():
        for h in heads:
            gift(0, h).wait_send()
            pl.when(place > 0)(lambda: gift(1, h).wait_send())

    @pl.when((odd == 1) & (place < scans - 1))
    def _():
        for h in heads:
            chain(h, 1).wait_send()
            pl.when(place < scans - 2)(lambda: chain(h, 2).wait_send())


def shards(*arrays):
    query_row, gain_row = arrays[0], arrays[5]
    lines, scans = lax.axis_size("line"), lax.axis_size("scan")
    tokens, features = query_row.shape[1:]
    size = gain_row.shape[0]
    heads = features // size
    groups = 2 if heads % 2 == 0 else 1
    arrays = list(arrays)
    arrays[5] = arrays[5].reshape(1, size)
    arrays[10] = arrays[10].reshape(1, size)
    square = (heads, size, size)
    rows = (heads, tokens, size)
    swapped = (groups, lines, heads // groups, tokens // lines, size)
    dma = pltpu.SemaphoreType.DMA
    return pl.pallas_call(
        functools.partial(kernel, lines, scans),
        out_shape=jax.ShapeDtypeStruct(query_row.shape, BF16),
        in_specs=[pl.BlockSpec(memory_space=pl.ANY)] * len(arrays),
        out_specs=pl.BlockSpec(memory_space=pltpu.VMEM),
        scratch_shapes=[pltpu.VMEM(a.shape, a.dtype) for a in arrays]
        + [
            pltpu.VMEM(square, BF16),
            pltpu.VMEM((heads, tokens, 2 * size), F32),
            pltpu.VMEM((2,) + square, BF16),
            pltpu.VMEM((2,) + square, BF16),
            pltpu.VMEM(square, BF16),
            pltpu.VMEM(square, BF16),
            pltpu.VMEM(square, F32),
            pltpu.VMEM(square, F32),
            pltpu.VMEM(rows, F32),
            pltpu.VMEM(rows, F32),
            pltpu.VMEM(rows, F32),
            pltpu.VMEM(swapped, BF16),
            pltpu.VMEM(swapped, BF16),
            pltpu.VMEM(swapped, BF16),
            pltpu.VMEM(swapped, BF16),
            dma((len(arrays),)),
            dma((2, heads)),
            dma((2, heads)),
            dma((2, heads)),
            dma((heads,)),
            dma((groups, lines)),
            dma((groups, lines)),
            dma((groups, lines)),
            dma((groups, lines)),
        ],
        compiler_params=pltpu.CompilerParams(
            collective_id=0, has_side_effects=True, vmem_limit_bytes=56 * 1024 * 1024
        ),
    )(*arrays)


def solution(mesh):
    placed = (
        P("line", "scan", None),
        P("line", "scan", None),
        P("line", "scan", None),
        P("line", "scan", None),
        P("line", "scan", None),
        P(),
        P(None, "scan", "line", None),
        P(None, "scan", "line", None),
        P(None, "scan", "line", None),
        P(None, "scan", "line", None),
        P(),
    )
    return jax.shard_map(
        shards, mesh=mesh, in_specs=placed, out_specs=P("line", "scan", None), check_vma=False
    )
```

```python
import functools

import jax
import jax.numpy as jnp
from jax import lax
from jax.experimental import pallas as pl
from jax.experimental.pallas import tpu as pltpu
from jax.sharding import PartitionSpec as P

F32 = jnp.float32
BF16 = jnp.bfloat16


def dot(a, b):
    return jnp.dot(a, b, preferred_element_type=F32)


def dot_t(a, b):
    return lax.dot_general(a, b, (((1,), (1,)), ((), ())), preferred_element_type=F32)


def split(a):
    high = a.astype(BF16)
    return high, (a - high.astype(F32)).astype(BF16)


def dot_left(a, b):
    high, low = split(a)
    return dot(high, b) + dot(low, b)


def dot_right(a, b):
    high, low = split(b)
    return dot(a, high) + dot(a, low)


def dot_pairs(a, b):
    return dot(a[0], b[0]) + (dot(a[0], b[1]) + dot(a[1], b[0]))


def masks(size, stride):
    row = lax.broadcasted_iota(jnp.int32, (size, size), 0)
    col = lax.broadcasted_iota(jnp.int32, (size, size), 1)
    same = lax.rem(row, stride) == lax.rem(col, stride)
    return row, col, row == col, same & (row >= col), same & (row > col)


def to_row(column, diagonal):
    return jnp.sum(jnp.where(diagonal, column, 0.0), axis=0, keepdims=True)


def dot16(a, b):
    return dot(a.astype(BF16), b.astype(BF16))


def inverse(systems, row, col, diagonal, stride, steps, refine):
    unit = jnp.where(diagonal, 1.0, 0.0)
    base = min(16, steps)
    near = (row // (base * stride)) == (col // (base * stride))
    power = [jnp.where(near, m, 0.0) for m in systems]
    total = [unit - m for m in power]
    reach = 2
    while reach < base:
        power = [dot16(m, m) for m in power]
        total = [t + dot16(t, m) for t, m in zip(total, power)]
        reach *= 2
    size = base
    while size < steps:
        wide = size * 2 * stride
        link = ((row // wide) == (col // wide)) & (
            (row // (size * stride)) != (col // (size * stride))
        )
        inner = [dot16(jnp.where(link, m, 0.0), t) for m, t in zip(systems, total)]
        total = [t - dot16(t, i) for t, i in zip(total, inner)]
        size *= 2
    if refine:
        left = [
            (unit - t) - dot_pairs(split(m), split(t)) for m, t in zip(systems, total)
        ]
        total = [t + dot16(t, e) for t, e in zip(total, left)]
    return total


def prepare(queries, keys, decay, beta, stride, refine):
    size = keys[0].shape[0]
    steps = size // stride
    count = len(keys)
    row, col, diagonal, lower, strict = masks(size, stride)
    rest, cumulative = decay, 0.0
    upper = jnp.where(
        (lax.rem(row, stride) == lax.rem(col, stride)) & (row <= col), 1.0, 0.0
    ).astype(BF16)
    for _ in range(3):
        piece = rest.astype(BF16)
        rest = rest - piece.astype(F32)
        cumulative = cumulative + dot(piece, upper)
    packed = jnp.concatenate([cumulative, beta], axis=0).T
    cum_rows = [cumulative[h : h + 1] for h in range(count)]
    beta_rows = [beta[h : h + 1] for h in range(count)]
    cums = [packed[:, h : h + 1] for h in range(count)]
    systems, attends, units, unit_rows = [], [], [], []
    for h in range(count):
        gram = dot_t(keys[h], keys[h])
        squares = jnp.where(diagonal, gram, 0.0)
        unit_col = lax.rsqrt(jnp.sum(squares, axis=1, keepdims=True) + 1e-06)
        unit_row = lax.rsqrt(jnp.sum(squares, axis=0, keepdims=True) + 1e-06)
        spread = cums[h] - cum_rows[h]
        ratio = jnp.where(lower, jnp.exp(jnp.where(lower, spread, 0.0)), 0.0) * unit_row
        beta_col = packed[:, count + h : count + h + 1]
        systems.append(jnp.where(strict, (beta_col * unit_col) * (ratio * gram), 0.0))
        attends.append(ratio * dot_t(queries[h], keys[h]))
        units.append(unit_col)
        unit_rows.append(unit_row)
    solved = inverse(systems, row, col, diagonal, stride, steps, refine)
    return solved, attends, cums, units, cum_rows, beta_rows, unit_rows, diagonal


def normed(block, gain):
    return block * lax.rsqrt(jnp.mean(block * block, axis=-1, keepdims=True) + 1e-05) * gain


def each(count, body):
    if count <= 8:
        for i in range(count):
            body(i)
    else:
        lax.fori_loop(0, count, lambda i, c: (body(i), c)[1], 0)


def kernel(
    lines,
    scans,
    *refs,
):
    hbm, out, held = refs[:11], refs[11], refs[12:23]
    (
        state,
        gift_out,
        gift_in,
        chain_out,
        chain_in,
        offset,
        local,
        asking,
        mixer,
        outgoing,
        incoming,
        returning,
        returned,
        load_sem,
        gift_send,
        gift_recv,
        chain_send,
        chain_recv,
        there_send,
        there_recv,
        back_send,
        back_recv,
    ) = refs[23:]
    (
        query_row,
        key_row,
        value_row,
        decay_row,
        beta_row,
        gain_row,
        query_col,
        key_col,
        decay_col,
        beta_col,
        gain_col,
    ) = held
    me = lax.axis_index("line")
    place = lax.axis_index("scan")
    odd = lax.rem(place, 2)
    tokens, features = query_row.shape[1:]
    size = gain_row.shape[1]
    heads = range(features // size)
    total_rows, width = query_col.shape[0], query_col.shape[2]
    groups = outgoing.shape[0]
    group_heads = outgoing.shape[2]
    mesh_id = pl.DeviceIdType.MESH

    def load(i):
        return pltpu.make_async_copy(hbm[i], held[i], load_sem.at[i])

    for i in (1, 3, 4, 0, 2, 5, 7, 6, 8, 9, 10):
        load(i).start()

    barrier = pltpu.get_barrier_semaphore()

    def greet(i):
        pl.semaphore_signal(
            barrier, inc=1, device_id={"line": lax.rem(me + 1 + i, lines)}, device_id_type=mesh_id
        )

    each(lines - 1, greet)

    def greet_along(distance):
        pl.semaphore_signal(
            barrier, inc=1, device_id={"scan": place + distance}, device_id_type=mesh_id
        )

    pl.when(place > 0)(lambda: greet_along(-1))
    pl.when(place < scans - 1)(lambda: greet_along(1))
    pl.when((odd == 1) & (place > 1))(lambda: greet_along(-2))
    pl.when((odd == 1) & (place < scans - 2))(lambda: greet_along(2))

    def of_head(ref, h):
        return ref[0, :, h * size : (h + 1) * size]

    for i in (1, 3, 4, 0):
        load(i).wait()
    queries = [of_head(query_row, h) for h in heads]
    keys = [of_head(key_row, h) for h in heads]
    solved, attends, cums, units, cum_rows, beta_rows, unit_rows, diagonal = prepare(
        queries, keys, decay_row[0], beta_row[0], 1, True
    )
    load(2).wait()
    pl.semaphore_wait(
        barrier,
        lines
        - 1
        + jnp.minimum(place, 1)
        + jnp.minimum(scans - 1 - place, 1)
        + odd * (jnp.minimum(place // 2, 1) + jnp.minimum((scans - 1 - place) // 2, 1)),
    )

    def gift(which, g):
        return pltpu.make_async_remote_copy(
            src_ref=gift_out.at[which, g],
            dst_ref=gift_in.at[which, g],
            send_sem=gift_send.at[which, g],
            recv_sem=gift_recv.at[which, g],
            device_id={"scan": lax.rem(place + 1, scans)},
            device_id_type=mesh_id,
        )

    def chain(g, distance):
        return pltpu.make_async_remote_copy(
            src_ref=chain_out.at[g],
            dst_ref=chain_in.at[g],
            send_sem=chain_send.at[distance - 1, g],
            recv_sem=chain_recv.at[g],
            device_id={"scan": lax.rem(place + distance, scans)},
            device_id_type=mesh_id,
        )

    gives = (odd == 0) & (place < scans - 1)
    lasts = [c[tokens - 1 : tokens, :] for c in cums]
    tails = [jnp.exp(lasts[h] - cums[h]) * units[h] for h in heads]
    keys_t = [k.astype(F32).T.astype(BF16) for k in keys]
    updates, weighted = {}, {}
    for g in range(groups):
        for j in range(group_heads):
            h = g * group_heads + j
            updates[h] = dot_left(solved[h] * beta_rows[h], of_head(value_row, h))
            offset[h] = dot(keys_t[h], (tails[h] * updates[h]).astype(BF16))
            gift_out[0, g, j] = offset[h].astype(BF16)
        pl.when(gives)(lambda: gift(0, g).start())
    for h in heads:
        weighted[h] = dot_left(
            solved[h] * (beta_rows[h] * jnp.exp(cum_rows[h]) * unit_rows[h]), keys[h]
        )
        kept = dot(keys_t[h], (tails[h] * weighted[h]).astype(BF16))
        gift_out[1, h // group_heads, h % group_heads] = (
            jnp.where(diagonal, jnp.exp(lasts[h]), 0.0) - kept
        ).astype(BF16)

    @pl.when(gives & (place > 0))
    def _():
        for g in range(groups):
            gift(1, g).start()

    for h in heads:
        seen = dot_pairs(
            split(attends[h]), split(jnp.concatenate([updates[h], weighted[h]], axis=1))
        )
        local[h] = seen[:, :size]
        asking[h] = (
            jnp.exp(cums[h]) * queries[h].astype(F32) - seen[:, size:]
        ).astype(BF16)

    for i in (5, 7, 6, 8, 9, 10):
        load(i).wait()

    def of_head_col(ref, h):
        block = ref[:, 0, :, h * size : (h + 1) * size]
        return block.reshape(total_rows * width, size)

    def column_gates(ref):
        return jnp.concatenate([ref[t, 0] for t in range(total_rows)], axis=1)

    def column_terms():
        col_solved, col_attends, _, _, _, col_betas, _, _ = prepare(
            [of_head_col(query_col, h) for h in heads],
            [of_head_col(key_col, h) for h in heads],
            column_gates(decay_col),
            column_gates(beta_col),
            width,
            False,
        )
        for h in heads:
            mixer[0, h], mixer[1, h] = split(
                dot_pairs(split(col_attends[h]), split(col_solved[h] * col_betas[h]))
            )

    pl.when(place >= 2)(column_terms)

    @pl.when(place == 0)
    def _():
        state[...] = jnp.zeros_like(state)

    @pl.when(odd == 1)
    def _():
        for g in range(groups):
            gift(0, g).wait_recv()

            @pl.when(place == 1)
            def _():
                state[g] = gift_in[0, g]

            @pl.when(place > 1)
            def _():
                gift(1, g).wait_recv()
                chain(g, 1).wait_recv()
                for j in range(group_heads):
                    state[g, j] = (
                        dot(gift_in[1, g, j], chain_in[g, j]) + gift_in[0, g, j].astype(F32)
                    ).astype(BF16)

            @pl.when(place < scans - 1)
            def _():
                for j in range(group_heads):
                    chain_out[g, j] = (
                        dot(gift_out[1, g, j], state[g, j]) + offset[g * group_heads + j]
                    ).astype(BF16)
                chain(g, 1).start()
                pl.when(place < scans - 2)(lambda: chain(g, 2).start())

    @pl.when((odd == 0) & (place > 0))
    def _():
        for g in range(groups):
            chain(g, 1).wait_recv()
            state[g] = chain_in[g]

    def swap(source, target, send, recv, g, i):
        peer = lax.rem(me + 1 + i, lines)
        return pltpu.make_async_remote_copy(
            src_ref=source.at[g, peer],
            dst_ref=target.at[g, me],
            send_sem=send.at[g, i],
            recv_sem=recv.at[g, me],
            device_id={"line": peer},
            device_id_type=mesh_id,
        )

    def receive(source, target, send, recv, g, i):
        peer = lax.rem(me + 1 + i, lines)
        pltpu.make_async_remote_copy(
            src_ref=source.at[g, peer],
            dst_ref=target.at[g, peer],
            send_sem=send.at[g, i],
            recv_sem=recv.at[g, peer],
            device_id={"line": peer},
            device_id_type=mesh_id,
        ).wait_recv()

    there = (outgoing, incoming, there_send, there_recv)
    back = (returning, returned, back_send, back_recv)

    for g in range(groups):
        for j in range(group_heads):
            h = g * group_heads + j
            row_out = local[h] + dot(asking[h], state[g, j])
            values = normed(row_out, gain_row[...]).astype(BF16)
            outgoing[g, :, j] = values.reshape(lines, tokens // lines, size)
        each(lines - 1, lambda i: swap(*there, g, i).start())
        incoming[g, me] = outgoing[g, me]

    pl.when(place < 2)(column_terms)

    for g in range(groups):
        each(lines - 1, lambda i: receive(*there, g, i))
        for j in range(group_heads):
            h = g * group_heads + j
            values = incoming[g, :, j].reshape(total_rows * width, size)
            mixed = normed(
                dot(mixer[0, h], values) + dot(mixer[1, h], values), gain_col[...]
            ).astype(BF16)
            returning[g, :, j] = mixed.reshape(total_rows, width, size)
        each(lines - 1, lambda i: swap(*back, g, i).start())
        returned[g, me] = returning[g, me]

    for g in range(groups):
        each(lines - 1, lambda i: receive(*back, g, i))
        for j in range(group_heads):
            h = g * group_heads + j
            out[0, :, h * size : (h + 1) * size] = returned[g, :, j].reshape(tokens, size)

    for g in range(groups):
        each(lines - 1, lambda i: swap(*there, g, i).wait_send())
        each(lines - 1, lambda i: swap(*back, g, i).wait_send())

    @pl.when(gives)
    def _():
        for g in range(groups):
            gift(0, g).wait_send()
            pl.when(place > 0)(lambda: gift(1, g).wait_send())

    @pl.when((odd == 1) & (place < scans - 1))
    def _():
        for g in range(groups):
            chain(g, 1).wait_send()
            pl.when(place < scans - 2)(lambda: chain(g, 2).wait_send())


def shards(*arrays):
    query_row, gain_row = arrays[0], arrays[5]
    lines, scans = lax.axis_size("line"), lax.axis_size("scan")
    tokens, features = query_row.shape[1:]
    size = gain_row.shape[0]
    heads = features // size
    groups = 2 if heads % 2 == 0 else 1
    arrays = list(arrays)
    arrays[5] = arrays[5].reshape(1, size)
    arrays[10] = arrays[10].reshape(1, size)
    for i in (3, 4):
        arrays[i] = arrays[i].transpose(0, 2, 1)
    for i in (8, 9):
        arrays[i] = arrays[i].transpose(0, 1, 3, 2)
    grouped = (groups, heads // groups, size, size)
    swapped = (groups, lines, heads // groups, tokens // lines, size)
    dma = pltpu.SemaphoreType.DMA
    return pl.pallas_call(
        functools.partial(kernel, lines, scans),
        out_shape=jax.ShapeDtypeStruct(query_row.shape, BF16),
        in_specs=[pl.BlockSpec(memory_space=pltpu.HBM)] * len(arrays),
        out_specs=pl.BlockSpec(memory_space=pltpu.VMEM),
        scratch_shapes=[pltpu.VMEM(a.shape, a.dtype) for a in arrays]
        + [
            pltpu.VMEM(grouped, BF16),
            pltpu.VMEM((2,) + grouped, BF16),
            pltpu.VMEM((2,) + grouped, BF16),
            pltpu.VMEM(grouped, BF16),
            pltpu.VMEM(grouped, BF16),
            pltpu.VMEM((heads, size, size), F32),
            pltpu.VMEM((heads, tokens, size), F32),
            pltpu.VMEM((heads, tokens, size), BF16),
            pltpu.VMEM((2, heads, tokens, tokens), BF16),
            pltpu.VMEM(swapped, BF16),
            pltpu.VMEM(swapped, BF16),
            pltpu.VMEM(swapped, BF16),
            pltpu.VMEM(swapped, BF16),
            dma((len(arrays),)),
            dma((2, groups)),
            dma((2, groups)),
            dma((2, groups)),
            dma((groups,)),
            dma((groups, lines)),
            dma((groups, lines)),
            dma((groups, lines)),
            dma((groups, lines)),
        ],
        compiler_params=pltpu.CompilerParams(
            collective_id=0, has_side_effects=True, vmem_limit_bytes=60 * 1024 * 1024
        ),
    )(*arrays)


def solution(mesh):
    placed = (
        P("line", "scan", None),
        P("line", "scan", None),
        P("line", "scan", None),
        P("line", "scan", None),
        P("line", "scan", None),
        P(),
        P(None, "scan", "line", None),
        P(None, "scan", "line", None),
        P(None, "scan", "line", None),
        P(None, "scan", "line", None),
        P(),
    )
    return jax.shard_map(
        shards, mesh=mesh, in_specs=placed, out_specs=P("line", "scan", None), check_vma=False
    )
```

```python
import functools

import jax
import jax.numpy as jnp
from jax import lax
from jax.experimental import pallas as pl
from jax.experimental.pallas import tpu as pltpu
from jax.sharding import PartitionSpec as P

F32 = jnp.float32
BF16 = jnp.bfloat16


def dot(a, b):
    return jnp.dot(a, b, preferred_element_type=F32)


def dot_t(a, b):
    return lax.dot_general(a, b, (((1,), (1,)), ((), ())), preferred_element_type=F32)


def split(a):
    high = a.astype(BF16)
    return high, (a - high.astype(F32)).astype(BF16)


def dot_left(a, b):
    high, low = split(a)
    return dot(high, b) + dot(low, b)


def dot_right(a, b):
    high, low = split(b)
    return dot(a, high) + dot(a, low)


def dot_pairs(a, b):
    return dot(a[0], b[0]) + (dot(a[0], b[1]) + dot(a[1], b[0]))


def masks(size, stride):
    row = lax.broadcasted_iota(jnp.int32, (size, size), 0)
    col = lax.broadcasted_iota(jnp.int32, (size, size), 1)
    same = lax.rem(row, stride) == lax.rem(col, stride)
    return row, col, row == col, same & (row >= col), same & (row > col)


def to_row(column, diagonal):
    return jnp.sum(jnp.where(diagonal, column, 0.0), axis=0, keepdims=True)


def dot16(a, b):
    return dot(a.astype(BF16), b.astype(BF16))


def inverse(systems, row, col, diagonal, stride, steps, refine):
    unit = jnp.where(diagonal, 1.0, 0.0)
    base = min(16, steps)
    near = (row // (base * stride)) == (col // (base * stride))
    power = [jnp.where(near, m, 0.0) for m in systems]
    total = [unit - m for m in power]
    reach = 2
    while reach < base:
        power = [dot16(m, m) for m in power]
        total = [t + dot16(t, m) for t, m in zip(total, power)]
        reach *= 2
    size = base
    while size < steps:
        wide = size * 2 * stride
        link = ((row // wide) == (col // wide)) & (
            (row // (size * stride)) != (col // (size * stride))
        )
        inner = [dot16(jnp.where(link, m, 0.0), t) for m, t in zip(systems, total)]
        total = [t - dot16(t, i) for t, i in zip(total, inner)]
        size *= 2
    if refine:
        left = [
            (unit - t) - dot_pairs(split(m), split(t)) for m, t in zip(systems, total)
        ]
        total = [t + dot16(t, e) for t, e in zip(total, left)]
    return total


def prepare(queries, keys, decay, beta, stride, refine):
    size = keys[0].shape[0]
    steps = size // stride
    count = len(keys)
    row, col, diagonal, lower, strict = masks(size, stride)
    rest, cumulative = decay, 0.0
    upper = jnp.where(
        (lax.rem(row, stride) == lax.rem(col, stride)) & (row <= col), 1.0, 0.0
    ).astype(BF16)
    for _ in range(3):
        piece = rest.astype(BF16)
        rest = rest - piece.astype(F32)
        cumulative = cumulative + dot(piece, upper)
    packed = jnp.concatenate([cumulative, beta], axis=0).T
    cum_rows = [cumulative[h : h + 1] for h in range(count)]
    beta_rows = [beta[h : h + 1] for h in range(count)]
    cums = [packed[:, h : h + 1] for h in range(count)]
    systems, attends, units, unit_rows = [], [], [], []
    for h in range(count):
        gram = dot_t(keys[h], keys[h])
        squares = jnp.where(diagonal, gram, 0.0)
        unit_col = lax.rsqrt(jnp.sum(squares, axis=1, keepdims=True) + 1e-06)
        unit_row = lax.rsqrt(jnp.sum(squares, axis=0, keepdims=True) + 1e-06)
        spread = cums[h] - cum_rows[h]
        ratio = jnp.where(lower, jnp.exp(jnp.where(lower, spread, 0.0)), 0.0) * unit_row
        beta_col = packed[:, count + h : count + h + 1]
        systems.append(jnp.where(strict, (beta_col * unit_col) * (ratio * gram), 0.0))
        attends.append(ratio * dot_t(queries[h], keys[h]))
        units.append(unit_col)
        unit_rows.append(unit_row)
    solved = inverse(systems, row, col, diagonal, stride, steps, refine)
    return solved, attends, cums, units, cum_rows, beta_rows, unit_rows, diagonal


def normed(block, gain):
    return block * lax.rsqrt(jnp.mean(block * block, axis=-1, keepdims=True) + 1e-05) * gain


def each(count, body):
    if count <= 8:
        for i in range(count):
            body(i)
    else:
        lax.fori_loop(0, count, lambda i, c: (body(i), c)[1], 0)


def kernel(
    lines,
    scans,
    *refs,
):
    hbm, out, held = refs[:11], refs[11], refs[12:23]
    (
        state,
        gift_out,
        gift_in,
        chain_out,
        chain_in,
        offset,
        local,
        asking,
        mixer,
        outgoing,
        incoming,
        returning,
        returned,
        load_sem,
        gift_send,
        gift_recv,
        chain_send,
        chain_recv,
        there_send,
        there_recv,
        back_send,
        back_recv,
    ) = refs[23:]
    (
        query_row,
        key_row,
        value_row,
        decay_row,
        beta_row,
        gain_row,
        query_col,
        key_col,
        decay_col,
        beta_col,
        gain_col,
    ) = held
    me = lax.axis_index("line")
    place = lax.axis_index("scan")
    odd = lax.rem(place, 2)
    tokens, features = query_row.shape[1:]
    size = gain_row.shape[1]
    heads = range(features // size)
    total_rows, width = query_col.shape[0], query_col.shape[2]
    groups = outgoing.shape[0]
    group_heads = outgoing.shape[2]
    mesh_id = pl.DeviceIdType.MESH

    def load(i):
        return pltpu.make_async_copy(hbm[i], held[i], load_sem.at[i])

    for i in (1, 3, 4, 0, 2, 5, 7, 6, 8, 9, 10):
        load(i).start()

    barrier = pltpu.get_barrier_semaphore()

    def greet(i):
        pl.semaphore_signal(
            barrier, inc=1, device_id={"line": lax.rem(me + 1 + i, lines)}, device_id_type=mesh_id
        )

    each(lines - 1, greet)

    def greet_along(distance):
        pl.semaphore_signal(
            barrier, inc=1, device_id={"scan": place + distance}, device_id_type=mesh_id
        )

    pl.when(place > 0)(lambda: greet_along(-1))
    pl.when(place < scans - 1)(lambda: greet_along(1))
    pl.when((odd == 1) & (place > 1))(lambda: greet_along(-2))
    pl.when((odd == 1) & (place < scans - 2))(lambda: greet_along(2))

    def of_head(ref, h):
        return ref[0, :, h * size : (h + 1) * size]

    for i in (1, 3, 4, 0):
        load(i).wait()
    queries = [of_head(query_row, h) for h in heads]
    keys = [of_head(key_row, h) for h in heads]
    solved, attends, cums, units, cum_rows, beta_rows, unit_rows, diagonal = prepare(
        queries, keys, decay_row[0], beta_row[0], 1, True
    )
    load(2).wait()
    pl.semaphore_wait(
        barrier,
        lines
        - 1
        + jnp.minimum(place, 1)
        + jnp.minimum(scans - 1 - place, 1)
        + odd * (jnp.minimum(place // 2, 1) + jnp.minimum((scans - 1 - place) // 2, 1)),
    )

    def gift(which, g):
        return pltpu.make_async_remote_copy(
            src_ref=gift_out.at[which, g],
            dst_ref=gift_in.at[which, g],
            send_sem=gift_send.at[which, g],
            recv_sem=gift_recv.at[which, g],
            device_id={"scan": lax.rem(place + 1, scans)},
            device_id_type=mesh_id,
        )

    def chain(g, distance):
        return pltpu.make_async_remote_copy(
            src_ref=chain_out.at[g],
            dst_ref=chain_in.at[g],
            send_sem=chain_send.at[distance - 1, g],
            recv_sem=chain_recv.at[g],
            device_id={"scan": lax.rem(place + distance, scans)},
            device_id_type=mesh_id,
        )

    gives = (odd == 0) & (place < scans - 1)
    lasts = [c[tokens - 1 : tokens, :] for c in cums]
    tails = [jnp.exp(lasts[h] - cums[h]) * units[h] for h in heads]
    keys_t = [k.astype(F32).T.astype(BF16) for k in keys]
    updates, weighted = {}, {}
    for g in range(groups):
        for j in range(group_heads):
            h = g * group_heads + j
            updates[h] = dot_left(solved[h] * beta_rows[h], of_head(value_row, h))
            offset[h] = dot(keys_t[h], (tails[h] * updates[h]).astype(BF16))
            gift_out[0, g, j] = offset[h].astype(BF16)
        pl.when(gives)(lambda: gift(0, g).start())
    for h in heads:
        weighted[h] = dot_left(
            solved[h] * (beta_rows[h] * jnp.exp(cum_rows[h]) * unit_rows[h]), keys[h]
        )
        kept = dot(keys_t[h], (tails[h] * weighted[h]).astype(BF16))
        gift_out[1, h // group_heads, h % group_heads] = (
            jnp.where(diagonal, jnp.exp(lasts[h]), 0.0) - kept
        ).astype(BF16)

    @pl.when(gives & (place > 0))
    def _():
        for g in range(groups):
            gift(1, g).start()

    for h in heads:
        seen = dot_pairs(
            split(attends[h]), split(jnp.concatenate([updates[h], weighted[h]], axis=1))
        )
        local[h] = seen[:, :size]
        asking[h] = (
            jnp.exp(cums[h]) * queries[h].astype(F32) - seen[:, size:]
        ).astype(BF16)

    for i in (5, 7, 6, 8, 9, 10):
        load(i).wait()

    def of_head_col(ref, h):
        block = ref[:, 0, :, h * size : (h + 1) * size]
        return block.reshape(total_rows * width, size)

    def column_gates(ref):
        return jnp.concatenate([ref[t, 0] for t in range(total_rows)], axis=1)

    def column_terms():
        col_solved, col_attends, _, _, _, col_betas, _, _ = prepare(
            [of_head_col(query_col, h) for h in heads],
            [of_head_col(key_col, h) for h in heads],
            column_gates(decay_col),
            column_gates(beta_col),
            width,
            False,
        )
        for h in heads:
            mixer[0, h], mixer[1, h] = split(
                dot_pairs(split(col_attends[h]), split(col_solved[h] * col_betas[h]))
            )

    pl.when(place >= 2)(column_terms)

    @pl.when(place == 0)
    def _():
        state[...] = jnp.zeros_like(state)

    def receive_state(g):
        @pl.when(odd == 1)
        def _():
            gift(0, g).wait_recv()

            @pl.when(place == 1)
            def _():
                state[g] = gift_in[0, g]

            @pl.when(place > 1)
            def _():
                gift(1, g).wait_recv()
                chain(g, 1).wait_recv()
                for j in range(group_heads):
                    state[g, j] = (
                        dot(gift_in[1, g, j], chain_in[g, j]) + gift_in[0, g, j].astype(F32)
                    ).astype(BF16)

            @pl.when(place < scans - 1)
            def _():
                for j in range(group_heads):
                    chain_out[g, j] = (
                        dot(gift_out[1, g, j], state[g, j]) + offset[g * group_heads + j]
                    ).astype(BF16)
                chain(g, 1).start()
                pl.when(place < scans - 2)(lambda: chain(g, 2).start())

        @pl.when((odd == 0) & (place > 0))
        def _():
            chain(g, 1).wait_recv()
            state[g] = chain_in[g]

    def swap(source, target, send, recv, g, i):
        peer = lax.rem(me + 1 + i, lines)
        return pltpu.make_async_remote_copy(
            src_ref=source.at[g, peer],
            dst_ref=target.at[g, me],
            send_sem=send.at[g, i],
            recv_sem=recv.at[g, me],
            device_id={"line": peer},
            device_id_type=mesh_id,
        )

    def receive(source, target, send, recv, g, i):
        peer = lax.rem(me + 1 + i, lines)
        pltpu.make_async_remote_copy(
            src_ref=source.at[g, peer],
            dst_ref=target.at[g, peer],
            send_sem=send.at[g, i],
            recv_sem=recv.at[g, peer],
            device_id={"line": peer},
            device_id_type=mesh_id,
        ).wait_recv()

    there = (outgoing, incoming, there_send, there_recv)
    back = (returning, returned, back_send, back_recv)

    for g in range(groups):
        receive_state(g)
        for j in range(group_heads):
            h = g * group_heads + j
            row_out = local[h] + dot(asking[h], state[g, j])
            values = normed(row_out, gain_row[...]).astype(BF16)
            outgoing[g, :, j] = values.reshape(lines, tokens // lines, size)
        each(lines - 1, lambda i: swap(*there, g, i).start())
        incoming[g, me] = outgoing[g, me]

    pl.when(place < 2)(column_terms)

    for g in range(groups):
        each(lines - 1, lambda i: receive(*there, g, i))
        for j in range(group_heads):
            h = g * group_heads + j
            values = incoming[g, :, j].reshape(total_rows * width, size)
            mixed = normed(
                dot(mixer[0, h], values) + dot(mixer[1, h], values), gain_col[...]
            ).astype(BF16)
            returning[g, :, j] = mixed.reshape(total_rows, width, size)
        each(lines - 1, lambda i: swap(*back, g, i).start())
        returned[g, me] = returning[g, me]

    for g in range(groups):
        each(lines - 1, lambda i: receive(*back, g, i))
        for j in range(group_heads):
            h = g * group_heads + j
            out[0, :, h * size : (h + 1) * size] = returned[g, :, j].reshape(tokens, size)

    for g in range(groups):
        each(lines - 1, lambda i: swap(*there, g, i).wait_send())
        each(lines - 1, lambda i: swap(*back, g, i).wait_send())

    @pl.when(gives)
    def _():
        for g in range(groups):
            gift(0, g).wait_send()
            pl.when(place > 0)(lambda: gift(1, g).wait_send())

    @pl.when((odd == 1) & (place < scans - 1))
    def _():
        for g in range(groups):
            chain(g, 1).wait_send()
            pl.when(place < scans - 2)(lambda: chain(g, 2).wait_send())


def shards(*arrays):
    query_row, gain_row = arrays[0], arrays[5]
    lines, scans = lax.axis_size("line"), lax.axis_size("scan")
    tokens, features = query_row.shape[1:]
    size = gain_row.shape[0]
    heads = features // size
    groups = heads
    arrays = list(arrays)
    arrays[5] = arrays[5].reshape(1, size)
    arrays[10] = arrays[10].reshape(1, size)
    for i in (3, 4):
        arrays[i] = arrays[i].transpose(0, 2, 1)
    for i in (8, 9):
        arrays[i] = arrays[i].transpose(0, 1, 3, 2)
    grouped = (groups, heads // groups, size, size)
    swapped = (groups, lines, heads // groups, tokens // lines, size)
    dma = pltpu.SemaphoreType.DMA
    return pl.pallas_call(
        functools.partial(kernel, lines, scans),
        out_shape=pltpu.VMEM(query_row.shape, BF16),
        in_specs=[pl.BlockSpec(memory_space=pltpu.HBM)] * len(arrays),
        out_specs=pl.BlockSpec(memory_space=pltpu.VMEM),
        scratch_shapes=[pltpu.VMEM(a.shape, a.dtype) for a in arrays]
        + [
            pltpu.VMEM(grouped, BF16),
            pltpu.VMEM((2,) + grouped, BF16),
            pltpu.VMEM((2,) + grouped, BF16),
            pltpu.VMEM(grouped, BF16),
            pltpu.VMEM(grouped, BF16),
            pltpu.VMEM((heads, size, size), F32),
            pltpu.VMEM((heads, tokens, size), F32),
            pltpu.VMEM((heads, tokens, size), BF16),
            pltpu.VMEM((2, heads, tokens, tokens), BF16),
            pltpu.VMEM(swapped, BF16),
            pltpu.VMEM(swapped, BF16),
            pltpu.VMEM(swapped, BF16),
            pltpu.VMEM(swapped, BF16),
            dma((len(arrays),)),
            dma((2, groups)),
            dma((2, groups)),
            dma((2, groups)),
            dma((groups,)),
            dma((groups, lines)),
            dma((groups, lines)),
            dma((groups, lines)),
            dma((groups, lines)),
        ],
        compiler_params=pltpu.CompilerParams(
            collective_id=0, has_side_effects=True, vmem_limit_bytes=60 * 1024 * 1024
        ),
    )(*arrays)


def solution(mesh):
    placed = (
        P("line", "scan", None),
        P("line", "scan", None),
        P("line", "scan", None),
        P("line", "scan", None),
        P("line", "scan", None),
        P(),
        P(None, "scan", "line", None),
        P(None, "scan", "line", None),
        P(None, "scan", "line", None),
        P(None, "scan", "line", None),
        P(),
    )
    return jax.shard_map(
        shards, mesh=mesh, in_specs=placed, out_specs=P("line", "scan", None), check_vma=False
    )
```

```python
import functools

import jax
import jax.numpy as jnp
from jax import lax
from jax.experimental import pallas as pl
from jax.experimental.pallas import tpu as pltpu
from jax.sharding import PartitionSpec as P

F32 = jnp.float32
BF16 = jnp.bfloat16


def dot(a, b):
    return jnp.dot(a, b, preferred_element_type=F32)


def dot_t(a, b):
    return lax.dot_general(a, b, (((1,), (1,)), ((), ())), preferred_element_type=F32)


def split(a):
    high = a.astype(BF16)
    return high, (a - high.astype(F32)).astype(BF16)


def dot_left(a, b):
    high, low = split(a)
    return dot(high, b) + dot(low, b)


def dot_right(a, b):
    high, low = split(b)
    return dot(a, high) + dot(a, low)


def dot_pairs(a, b):
    return dot(a[0], b[0]) + (dot(a[0], b[1]) + dot(a[1], b[0]))


def masks(size, stride):
    row = lax.broadcasted_iota(jnp.int32, (size, size), 0)
    col = lax.broadcasted_iota(jnp.int32, (size, size), 1)
    same = lax.rem(row, stride) == lax.rem(col, stride)
    return row, col, row == col, same & (row >= col), same & (row > col)


def to_row(column, diagonal):
    return jnp.sum(jnp.where(diagonal, column, 0.0), axis=0, keepdims=True)


def dot16(a, b):
    return dot(a.astype(BF16), b.astype(BF16))


def inverse(systems, row, col, diagonal, stride, steps, refine):
    unit = jnp.where(diagonal, 1.0, 0.0)
    base = min(16, steps)
    near = (row // (base * stride)) == (col // (base * stride))
    power = [jnp.where(near, m, 0.0) for m in systems]
    total = [unit - m for m in power]
    reach = 2
    while reach < base:
        power = [dot16(m, m) for m in power]
        total = [t + dot16(t, m) for t, m in zip(total, power)]
        reach *= 2
    size = base
    while size < steps:
        wide = size * 2 * stride
        link = ((row // wide) == (col // wide)) & (
            (row // (size * stride)) != (col // (size * stride))
        )
        inner = [dot16(jnp.where(link, m, 0.0), t) for m, t in zip(systems, total)]
        total = [t - dot16(t, i) for t, i in zip(total, inner)]
        size *= 2
    if refine:
        left = [
            (unit - t) - dot_pairs(split(m), split(t)) for m, t in zip(systems, total)
        ]
        total = [t + dot16(t, e) for t, e in zip(total, left)]
    return total


def prepare(queries, keys, decay, beta, stride, refine):
    size = keys[0].shape[0]
    steps = size // stride
    count = len(keys)
    row, col, diagonal, lower, strict = masks(size, stride)
    rest, cumulative = decay, 0.0
    upper = jnp.where(
        (lax.rem(row, stride) == lax.rem(col, stride)) & (row <= col), 1.0, 0.0
    ).astype(BF16)
    for _ in range(3):
        piece = rest.astype(BF16)
        rest = rest - piece.astype(F32)
        cumulative = cumulative + dot(piece, upper)
    packed = jnp.concatenate([cumulative, beta], axis=0).T
    cum_rows = [cumulative[h : h + 1] for h in range(count)]
    beta_rows = [beta[h : h + 1] for h in range(count)]
    cums = [packed[:, h : h + 1] for h in range(count)]
    systems, attends, units, unit_rows = [], [], [], []
    for h in range(count):
        gram = dot_t(keys[h], keys[h])
        squares = jnp.where(diagonal, gram, 0.0)
        unit_col = lax.rsqrt(jnp.sum(squares, axis=1, keepdims=True) + 1e-06)
        unit_row = lax.rsqrt(jnp.sum(squares, axis=0, keepdims=True) + 1e-06)
        spread = cums[h] - cum_rows[h]
        ratio = jnp.where(lower, jnp.exp(jnp.where(lower, spread, 0.0)), 0.0) * unit_row
        beta_col = packed[:, count + h : count + h + 1]
        systems.append(jnp.where(strict, (beta_col * unit_col) * (ratio * gram), 0.0))
        attends.append(ratio * dot_t(queries[h], keys[h]))
        units.append(unit_col)
        unit_rows.append(unit_row)
    solved = inverse(systems, row, col, diagonal, stride, steps, refine)
    return solved, attends, cums, units, cum_rows, beta_rows, unit_rows, diagonal


def normed(block, gain):
    return block * lax.rsqrt(jnp.mean(block * block, axis=-1, keepdims=True) + 1e-05) * gain


def each(count, body):
    if count <= 8:
        for i in range(count):
            body(i)
    else:
        lax.fori_loop(0, count, lambda i, c: (body(i), c)[1], 0)


def kernel(
    lines,
    scans,
    *refs,
):
    hbm, out, held = refs[:11], refs[11], refs[12:23]
    (
        state,
        gift_out,
        gift_in,
        chain_out,
        chain_in,
        offset,
        local,
        asking,
        mixer,
        outgoing,
        incoming,
        returning,
        returned,
        load_sem,
        gift_send,
        gift_recv,
        chain_send,
        chain_recv,
        there_send,
        there_recv,
        back_send,
        back_recv,
    ) = refs[23:]
    (
        query_row,
        key_row,
        value_row,
        decay_row,
        beta_row,
        gain_row,
        query_col,
        key_col,
        decay_col,
        beta_col,
        gain_col,
    ) = held
    me = lax.axis_index("line")
    place = lax.axis_index("scan")
    odd = lax.rem(place, 2)
    tokens, features = query_row.shape[1:]
    size = gain_row.shape[1]
    heads = range(features // size)
    total_rows, width = query_col.shape[0], query_col.shape[2]
    groups = outgoing.shape[0]
    group_heads = outgoing.shape[2]
    mesh_id = pl.DeviceIdType.MESH

    def load(i):
        return pltpu.make_async_copy(hbm[i], held[i], load_sem.at[i])

    for i in (1, 3, 4, 0, 2, 5, 7, 6, 8, 9, 10):
        load(i).start()

    barrier = pltpu.get_barrier_semaphore()

    def greet(i):
        pl.semaphore_signal(
            barrier, inc=1, device_id={"line": lax.rem(me + 1 + i, lines)}, device_id_type=mesh_id
        )

    each(lines - 1, greet)

    def greet_along(distance):
        pl.semaphore_signal(
            barrier, inc=1, device_id={"scan": place + distance}, device_id_type=mesh_id
        )

    pl.when(place > 0)(lambda: greet_along(-1))
    pl.when(place < scans - 1)(lambda: greet_along(1))
    pl.when((odd == 1) & (place > 1))(lambda: greet_along(-2))
    pl.when((odd == 1) & (place < scans - 2))(lambda: greet_along(2))

    def of_head(ref, h):
        return ref[0, :, h * size : (h + 1) * size]

    for i in (1, 3, 4, 0):
        load(i).wait()
    queries = [of_head(query_row, h) for h in heads]
    keys = [of_head(key_row, h) for h in heads]
    solved, attends, cums, units, cum_rows, beta_rows, unit_rows, diagonal = prepare(
        queries, keys, decay_row[0], beta_row[0], 1, True
    )
    load(2).wait()
    pl.semaphore_wait(
        barrier,
        lines
        - 1
        + jnp.minimum(place, 1)
        + jnp.minimum(scans - 1 - place, 1)
        + odd * (jnp.minimum(place // 2, 1) + jnp.minimum((scans - 1 - place) // 2, 1)),
    )

    def gift(which, g):
        return pltpu.make_async_remote_copy(
            src_ref=gift_out.at[which, g],
            dst_ref=gift_in.at[which, g],
            send_sem=gift_send.at[which, g],
            recv_sem=gift_recv.at[which, g],
            device_id={"scan": lax.rem(place + 1, scans)},
            device_id_type=mesh_id,
        )

    def chain(g, distance):
        return pltpu.make_async_remote_copy(
            src_ref=chain_out.at[g],
            dst_ref=chain_in.at[g],
            send_sem=chain_send.at[distance - 1, g],
            recv_sem=chain_recv.at[g],
            device_id={"scan": lax.rem(place + distance, scans)},
            device_id_type=mesh_id,
        )

    gives = (odd == 0) & (place < scans - 1)
    lasts = [c[tokens - 1 : tokens, :] for c in cums]
    tails = [jnp.exp(lasts[h] - cums[h]) * units[h] for h in heads]
    keys_t = [k.astype(F32).T.astype(BF16) for k in keys]
    updates = [
        dot_left(solved[h] * beta_rows[h], of_head(value_row, h)) for h in heads
    ]
    offsets = [dot(keys_t[h], (tails[h] * updates[h]).astype(BF16)) for h in heads]
    for h in heads:
        gift_out[0, h // group_heads, h % group_heads] = offsets[h].astype(BF16)

    @pl.when(gives)
    def _():
        for g in range(groups):
            gift(0, g).start()

    weighted = {}
    for h in heads:
        offset[h] = offsets[h]
    for h in heads:
        weighted[h] = dot_left(
            solved[h] * (beta_rows[h] * jnp.exp(cum_rows[h]) * unit_rows[h]), keys[h]
        )
        kept = dot(keys_t[h], (tails[h] * weighted[h]).astype(BF16))
        gift_out[1, h // group_heads, h % group_heads] = (
            jnp.where(diagonal, jnp.exp(lasts[h]), 0.0) - kept
        ).astype(BF16)

    @pl.when(gives & (place > 0))
    def _():
        for g in range(groups):
            gift(1, g).start()

    for h in heads:
        seen = dot_pairs(
            split(attends[h]), split(jnp.concatenate([updates[h], weighted[h]], axis=1))
        )
        local[h] = seen[:, :size]
        asking[h] = (
            jnp.exp(cums[h]) * queries[h].astype(F32) - seen[:, size:]
        ).astype(BF16)

    for i in (5, 7, 6, 8, 9, 10):
        load(i).wait()

    def of_head_col(ref, h):
        block = ref[:, 0, :, h * size : (h + 1) * size]
        return block.reshape(total_rows * width, size)

    def column_gates(ref):
        return jnp.concatenate([ref[t, 0] for t in range(total_rows)], axis=1)

    def column_terms():
        col_solved, col_attends, _, _, _, col_betas, _, _ = prepare(
            [of_head_col(query_col, h) for h in heads],
            [of_head_col(key_col, h) for h in heads],
            column_gates(decay_col),
            column_gates(beta_col),
            width,
            False,
        )
        for h in heads:
            mixer[0, h], mixer[1, h] = split(
                dot_pairs(split(col_attends[h]), split(col_solved[h] * col_betas[h]))
            )

    pl.when(place >= 2)(column_terms)

    @pl.when(place == 0)
    def _():
        state[...] = jnp.zeros_like(state)

    def receive_state(g):
        @pl.when(odd == 1)
        def _():
            gift(0, g).wait_recv()

            @pl.when(place == 1)
            def _():
                state[g] = gift_in[0, g]

            @pl.when(place > 1)
            def _():
                gift(1, g).wait_recv()
                chain(g, 1).wait_recv()
                for j in range(group_heads):
                    state[g, j] = (
                        dot(gift_in[1, g, j], chain_in[g, j]) + gift_in[0, g, j].astype(F32)
                    ).astype(BF16)

            @pl.when(place < scans - 1)
            def _():
                for j in range(group_heads):
                    chain_out[g, j] = (
                        dot(gift_out[1, g, j], state[g, j]) + offset[g * group_heads + j]
                    ).astype(BF16)
                chain(g, 1).start()
                pl.when(place < scans - 2)(lambda: chain(g, 2).start())

        @pl.when((odd == 0) & (place > 0))
        def _():
            chain(g, 1).wait_recv()
            state[g] = chain_in[g]

    def swap(source, target, send, recv, g, i):
        peer = lax.rem(me + 1 + i, lines)
        return pltpu.make_async_remote_copy(
            src_ref=source.at[g, peer],
            dst_ref=target.at[g, me],
            send_sem=send.at[g, i],
            recv_sem=recv.at[g, me],
            device_id={"line": peer},
            device_id_type=mesh_id,
        )

    def receive(source, target, send, recv, g, i):
        peer = lax.rem(me + 1 + i, lines)
        pltpu.make_async_remote_copy(
            src_ref=source.at[g, peer],
            dst_ref=target.at[g, peer],
            send_sem=send.at[g, i],
            recv_sem=recv.at[g, peer],
            device_id={"line": peer},
            device_id_type=mesh_id,
        ).wait_recv()

    there = (outgoing, incoming, there_send, there_recv)
    back = (returning, returned, back_send, back_recv)

    for g in range(groups):
        receive_state(g)
        for j in range(group_heads):
            h = g * group_heads + j
            row_out = local[h] + dot(asking[h], state[g, j])
            values = normed(row_out, gain_row[...]).astype(BF16)
            outgoing[g, :, j] = values.reshape(lines, tokens // lines, size)
        each(lines - 1, lambda i: swap(*there, g, i).start())
        incoming[g, me] = outgoing[g, me]

    pl.when(place < 2)(column_terms)

    for g in range(groups):
        each(lines - 1, lambda i: receive(*there, g, i))
        for j in range(group_heads):
            h = g * group_heads + j
            values = incoming[g, :, j].reshape(total_rows * width, size)
            mixed = normed(
                dot(mixer[0, h], values) + dot(mixer[1, h], values), gain_col[...]
            ).astype(BF16)
            returning[g, :, j] = mixed.reshape(total_rows, width, size)
        each(lines - 1, lambda i: swap(*back, g, i).start())
        returned[g, me] = returning[g, me]

    for g in range(groups):
        each(lines - 1, lambda i: receive(*back, g, i))
        for j in range(group_heads):
            h = g * group_heads + j
            out[0, :, h * size : (h + 1) * size] = returned[g, :, j].reshape(tokens, size)

    for g in range(groups):
        each(lines - 1, lambda i: swap(*there, g, i).wait_send())
        each(lines - 1, lambda i: swap(*back, g, i).wait_send())

    @pl.when(gives)
    def _():
        for g in range(groups):
            gift(0, g).wait_send()
            pl.when(place > 0)(lambda: gift(1, g).wait_send())

    @pl.when((odd == 1) & (place < scans - 1))
    def _():
        for g in range(groups):
            chain(g, 1).wait_send()
            pl.when(place < scans - 2)(lambda: chain(g, 2).wait_send())


def shards(*arrays):
    query_row, gain_row = arrays[0], arrays[5]
    lines, scans = lax.axis_size("line"), lax.axis_size("scan")
    tokens, features = query_row.shape[1:]
    size = gain_row.shape[0]
    heads = features // size
    groups = heads
    arrays = list(arrays)
    arrays[5] = arrays[5].reshape(1, size)
    arrays[10] = arrays[10].reshape(1, size)
    for i in (3, 4):
        arrays[i] = arrays[i].transpose(0, 2, 1)
    for i in (8, 9):
        arrays[i] = arrays[i].transpose(0, 1, 3, 2)
    grouped = (groups, heads // groups, size, size)
    swapped = (groups, lines, heads // groups, tokens // lines, size)
    dma = pltpu.SemaphoreType.DMA
    return pl.pallas_call(
        functools.partial(kernel, lines, scans),
        out_shape=pltpu.VMEM(query_row.shape, BF16),
        in_specs=[pl.BlockSpec(memory_space=pltpu.HBM)] * len(arrays),
        out_specs=pl.BlockSpec(memory_space=pltpu.VMEM),
        scratch_shapes=[pltpu.VMEM(a.shape, a.dtype) for a in arrays]
        + [
            pltpu.VMEM(grouped, BF16),
            pltpu.VMEM((2,) + grouped, BF16),
            pltpu.VMEM((2,) + grouped, BF16),
            pltpu.VMEM(grouped, BF16),
            pltpu.VMEM(grouped, BF16),
            pltpu.VMEM((heads, size, size), F32),
            pltpu.VMEM((heads, tokens, size), F32),
            pltpu.VMEM((heads, tokens, size), BF16),
            pltpu.VMEM((2, heads, tokens, tokens), BF16),
            pltpu.VMEM(swapped, BF16),
            pltpu.VMEM(swapped, BF16),
            pltpu.VMEM(swapped, BF16),
            pltpu.VMEM(swapped, BF16),
            dma((len(arrays),)),
            dma((2, groups)),
            dma((2, groups)),
            dma((2, groups)),
            dma((groups,)),
            dma((groups, lines)),
            dma((groups, lines)),
            dma((groups, lines)),
            dma((groups, lines)),
        ],
        compiler_params=pltpu.CompilerParams(
            collective_id=0, has_side_effects=True, vmem_limit_bytes=60 * 1024 * 1024
        ),
    )(*arrays)


def solution(mesh):
    placed = (
        P("line", "scan", None),
        P("line", "scan", None),
        P("line", "scan", None),
        P("line", "scan", None),
        P("line", "scan", None),
        P(),
        P(None, "scan", "line", None),
        P(None, "scan", "line", None),
        P(None, "scan", "line", None),
        P(None, "scan", "line", None),
        P(),
    )
    return jax.shard_map(
        shards, mesh=mesh, in_specs=placed, out_specs=P("line", "scan", None), check_vma=False
    )
```

```python
import functools

import jax
import jax.numpy as jnp
from jax import lax
from jax.experimental import pallas as pl
from jax.experimental.pallas import tpu as pltpu
from jax.sharding import PartitionSpec as P

F32 = jnp.float32
BF16 = jnp.bfloat16


def dot(a, b):
    return jnp.dot(a, b, preferred_element_type=F32)


def split(a):
    high = a.astype(BF16)
    return high, (a - high.astype(F32)).astype(BF16)


def dot_left(a, b):
    high, low = split(a)
    return dot(high, b) + dot(low, b)


def dot_right(a, b):
    high, low = split(b)
    return dot(a, high) + dot(a, low)


def dot_pairs(a, b):
    return dot(a[0], b[0]) + (dot(a[0], b[1]) + dot(a[1], b[0]))


def masks(size, stride):
    row = lax.broadcasted_iota(jnp.int32, (size, size), 0)
    col = lax.broadcasted_iota(jnp.int32, (size, size), 1)
    same = lax.rem(row, stride) == lax.rem(col, stride)
    return row, col, row == col, same & (row >= col), same & (row > col)


def to_row(column, diagonal):
    return jnp.sum(jnp.where(diagonal, column, 0.0), axis=0, keepdims=True)


def dot16(a, b):
    return dot(a.astype(BF16), b.astype(BF16))


def inverse(systems, row, col, diagonal, stride, steps):
    unit = jnp.where(diagonal, 1.0, 0.0)
    base = min(16, steps)
    near = (row // (base * stride)) == (col // (base * stride))
    power = [jnp.where(near, m, 0.0) for m in systems]
    total = [unit - m for m in power]
    reach = 2
    while reach < base:
        power = [dot16(m, m) for m in power]
        total = [t + dot16(t, m) for t, m in zip(total, power)]
        reach *= 2
    size = base
    while size < steps:
        wide = size * 2 * stride
        link = ((row // wide) == (col // wide)) & (
            (row // (size * stride)) != (col // (size * stride))
        )
        inner = [dot16(jnp.where(link, m, 0.0), t) for m, t in zip(systems, total)]
        total = [t - dot16(t, i) for t, i in zip(total, inner)]
        size *= 2
    return total


def prepare(keys, keys_t, decay, beta, stride):
    size = keys[0].shape[0]
    steps = size // stride
    count = len(keys)
    row, col, diagonal, lower, strict = masks(size, stride)
    rest, cumulative = decay, 0.0
    upper = jnp.where(
        (lax.rem(row, stride) == lax.rem(col, stride)) & (row <= col), 1.0, 0.0
    ).astype(BF16)
    for _ in range(3):
        piece = rest.astype(BF16)
        rest = rest - piece.astype(F32)
        cumulative = cumulative + dot(piece, upper)
    packed = jnp.concatenate([cumulative, beta], axis=0).T
    cum_rows = [cumulative[h : h + 1] for h in range(count)]
    beta_rows = [beta[h : h + 1] for h in range(count)]
    cums = [packed[:, h : h + 1] for h in range(count)]
    systems, ratios, units, unit_rows = [], [], [], []
    for h in range(count):
        gram = dot(keys[h], keys_t[h])
        squares = jnp.where(diagonal, gram, 0.0)
        unit_col = lax.rsqrt(jnp.sum(squares, axis=1, keepdims=True) + 1e-06)
        unit_row = lax.rsqrt(jnp.sum(squares, axis=0, keepdims=True) + 1e-06)
        spread = cums[h] - cum_rows[h]
        ratio = jnp.where(lower, jnp.exp(jnp.where(lower, spread, 0.0)), 0.0) * unit_row
        beta_col = packed[:, count + h : count + h + 1]
        systems.append(jnp.where(strict, (beta_col * unit_col) * (ratio * gram), 0.0))
        ratios.append(ratio)
        units.append(unit_col)
        unit_rows.append(unit_row)
    solved = inverse(systems, row, col, diagonal, stride, steps)
    return solved, ratios, cums, units, cum_rows, beta_rows, unit_rows, diagonal


def normed(block, gain):
    return block * lax.rsqrt(jnp.mean(block * block, axis=-1, keepdims=True) + 1e-05) * gain


def each(count, body):
    if count <= 8:
        for i in range(count):
            body(i)
    else:
        lax.fori_loop(0, count, lambda i, c: (body(i), c)[1], 0)


def kernel(
    lines,
    scans,
    *refs,
):
    hbm, out, held = refs[:11], refs[11], refs[12:23]
    (
        state,
        gift_out,
        gift_in,
        chain_out,
        chain_in,
        offset,
        local,
        asking,
        mixer,
        outgoing,
        incoming,
        returning,
        returned,
        load_sem,
        gift_send,
        gift_recv,
        chain_send,
        chain_recv,
        there_send,
        there_recv,
        back_send,
        back_recv,
    ) = refs[23:]
    (
        query_row,
        key_row,
        value_row,
        decay_row,
        beta_row,
        gain_row,
        query_col,
        key_col,
        decay_col,
        beta_col,
        gain_col,
    ) = held
    me = lax.axis_index("line")
    place = lax.axis_index("scan")
    odd = lax.rem(place, 2)
    tokens, features = query_row.shape[1:]
    size = gain_row.shape[1]
    heads = range(features // size)
    total_rows, width = query_col.shape[0], query_col.shape[2]
    groups = outgoing.shape[0]
    group_heads = outgoing.shape[2]
    mesh_id = pl.DeviceIdType.MESH

    def load(i):
        return pltpu.make_async_copy(hbm[i], held[i], load_sem.at[i])

    for i in (1, 3, 4, 0, 2, 5, 7, 6, 8, 9, 10):
        load(i).start()

    barrier = pltpu.get_barrier_semaphore()

    def greet(i):
        pl.semaphore_signal(
            barrier, inc=1, device_id={"line": lax.rem(me + 1 + i, lines)}, device_id_type=mesh_id
        )

    each(lines - 1, greet)

    def greet_along(distance):
        pl.semaphore_signal(
            barrier, inc=1, device_id={"scan": place + distance}, device_id_type=mesh_id
        )

    pl.when(place > 0)(lambda: greet_along(-1))
    pl.when(place < scans - 1)(lambda: greet_along(1))
    pl.when((odd == 1) & (place > 1))(lambda: greet_along(-2))
    pl.when((odd == 1) & (place < scans - 2))(lambda: greet_along(2))

    def of_head(ref, h):
        return ref[0, :, h * size : (h + 1) * size]

    for i in (1, 3, 4):
        load(i).wait()
    keys = [of_head(key_row, h) for h in heads]
    keys_t = [k.T for k in keys]
    solved, ratios, cums, units, cum_rows, beta_rows, unit_rows, diagonal = prepare(
        keys, keys_t, decay_row[0], beta_row[0], 1
    )
    load(2).wait()
    pl.semaphore_wait(
        barrier,
        lines
        - 1
        + jnp.minimum(place, 1)
        + jnp.minimum(scans - 1 - place, 1)
        + odd * (jnp.minimum(place // 2, 1) + jnp.minimum((scans - 1 - place) // 2, 1)),
    )

    def gift(which, g):
        return pltpu.make_async_remote_copy(
            src_ref=gift_out.at[which, g],
            dst_ref=gift_in.at[which, g],
            send_sem=gift_send.at[which, g],
            recv_sem=gift_recv.at[which, g],
            device_id={"scan": lax.rem(place + 1, scans)},
            device_id_type=mesh_id,
        )

    def chain(g, distance):
        return pltpu.make_async_remote_copy(
            src_ref=chain_out.at[g],
            dst_ref=chain_in.at[g],
            send_sem=chain_send.at[distance - 1, g],
            recv_sem=chain_recv.at[g],
            device_id={"scan": lax.rem(place + distance, scans)},
            device_id_type=mesh_id,
        )

    gives = (odd == 0) & (place < scans - 1)
    lasts = [c[tokens - 1 : tokens, :] for c in cums]
    tails = [jnp.exp(lasts[h] - cums[h]) * units[h] for h in heads]
    updates = [
        dot_left(solved[h] * beta_rows[h], of_head(value_row, h)) for h in heads
    ]
    offsets = [dot(keys_t[h], (tails[h] * updates[h]).astype(BF16)) for h in heads]
    for h in heads:
        gift_out[0, h // group_heads, h % group_heads] = offsets[h].astype(BF16)

    @pl.when(gives)
    def _():
        for g in range(groups):
            gift(0, g).start()

    weighted = {}
    for h in heads:
        offset[h] = offsets[h]
    for h in heads:
        weighted[h] = dot_left(
            solved[h] * (beta_rows[h] * jnp.exp(cum_rows[h]) * unit_rows[h]), keys[h]
        )
        kept = dot(keys_t[h], (tails[h] * weighted[h]).astype(BF16))
        gift_out[1, h // group_heads, h % group_heads] = (
            jnp.where(diagonal, jnp.exp(lasts[h]), 0.0) - kept
        ).astype(BF16)

    @pl.when(gives & (place > 0))
    def _():
        for g in range(groups):
            gift(1, g).start()

    load(0).wait()
    queries = [of_head(query_row, h) for h in heads]
    for h in heads:
        seen = dot_pairs(
            split(ratios[h] * dot(queries[h], keys_t[h])), split(jnp.concatenate([updates[h], weighted[h]], axis=1))
        )
        local[h] = seen[:, :size]
        asking[h] = (
            jnp.exp(cums[h]) * queries[h].astype(F32) - seen[:, size:]
        ).astype(BF16)

    for i in (5, 7, 6, 8, 9, 10):
        load(i).wait()

    def of_head_col(ref, h):
        block = ref[:, 0, :, h * size : (h + 1) * size]
        return block.reshape(total_rows * width, size)

    def column_gates(ref):
        return jnp.concatenate([ref[t, 0] for t in range(total_rows)], axis=1)

    def column_terms():
        col_keys = [of_head_col(key_col, h) for h in heads]
        col_keys_t = [k.T for k in col_keys]
        col_solved, col_ratios, _, _, _, col_betas, _, _ = prepare(
            col_keys, col_keys_t, column_gates(decay_col), column_gates(beta_col), width
        )
        for h in heads:
            attend = col_ratios[h] * dot(of_head_col(query_col, h), col_keys_t[h])
            mixer[0, h], mixer[1, h] = split(
                dot_pairs(split(attend), split(col_solved[h] * col_betas[h]))
            )

    pl.when(place >= 2)(column_terms)

    @pl.when(place == 0)
    def _():
        state[...] = jnp.zeros_like(state)

    def receive_state(g):
        @pl.when(odd == 1)
        def _():
            gift(0, g).wait_recv()

            @pl.when(place == 1)
            def _():
                state[g] = gift_in[0, g]

            @pl.when(place > 1)
            def _():
                gift(1, g).wait_recv()
                chain(g, 1).wait_recv()
                for j in range(group_heads):
                    state[g, j] = (
                        dot(gift_in[1, g, j], chain_in[g, j]) + gift_in[0, g, j].astype(F32)
                    ).astype(BF16)

            @pl.when(place < scans - 1)
            def _():
                for j in range(group_heads):
                    chain_out[g, j] = (
                        dot(gift_out[1, g, j], state[g, j]) + offset[g * group_heads + j]
                    ).astype(BF16)
                chain(g, 1).start()
                pl.when(place < scans - 2)(lambda: chain(g, 2).start())

        @pl.when((odd == 0) & (place > 0))
        def _():
            chain(g, 1).wait_recv()
            state[g] = chain_in[g]

    def swap(source, target, send, recv, g, i):
        peer = lax.rem(me + 1 + i, lines)
        return pltpu.make_async_remote_copy(
            src_ref=source.at[g, peer],
            dst_ref=target.at[g, me],
            send_sem=send.at[g, i],
            recv_sem=recv.at[g, me],
            device_id={"line": peer},
            device_id_type=mesh_id,
        )

    def receive(source, target, send, recv, g, i):
        peer = lax.rem(me + 1 + i, lines)
        pltpu.make_async_remote_copy(
            src_ref=source.at[g, peer],
            dst_ref=target.at[g, peer],
            send_sem=send.at[g, i],
            recv_sem=recv.at[g, peer],
            device_id={"line": peer},
            device_id_type=mesh_id,
        ).wait_recv()

    there = (outgoing, incoming, there_send, there_recv)
    back = (returning, returned, back_send, back_recv)

    for g in range(groups):
        receive_state(g)
        for j in range(group_heads):
            h = g * group_heads + j
            row_out = local[h] + dot(asking[h], state[g, j])
            values = normed(row_out, gain_row[...]).astype(BF16)
            outgoing[g, :, j] = values.reshape(lines, tokens // lines, size)
        each(lines - 1, lambda i: swap(*there, g, i).start())
        incoming[g, me] = outgoing[g, me]

    pl.when(place < 2)(column_terms)

    for g in range(groups):
        each(lines - 1, lambda i: receive(*there, g, i))
        for j in range(group_heads):
            h = g * group_heads + j
            values = incoming[g, :, j].reshape(total_rows * width, size)
            mixed = normed(
                dot(mixer[0, h], values) + dot(mixer[1, h], values), gain_col[...]
            ).astype(BF16)
            returning[g, :, j] = mixed.reshape(total_rows, width, size)
        each(lines - 1, lambda i: swap(*back, g, i).start())
        returned[g, me] = returning[g, me]

    for g in range(groups):
        each(lines - 1, lambda i: receive(*back, g, i))
        for j in range(group_heads):
            h = g * group_heads + j
            out[0, :, h * size : (h + 1) * size] = returned[g, :, j].reshape(tokens, size)

    for g in range(groups):
        each(lines - 1, lambda i: swap(*there, g, i).wait_send())
        each(lines - 1, lambda i: swap(*back, g, i).wait_send())

    @pl.when(gives)
    def _():
        for g in range(groups):
            gift(0, g).wait_send()
            pl.when(place > 0)(lambda: gift(1, g).wait_send())

    @pl.when((odd == 1) & (place < scans - 1))
    def _():
        for g in range(groups):
            chain(g, 1).wait_send()
            pl.when(place < scans - 2)(lambda: chain(g, 2).wait_send())


def shards(*arrays):
    query_row, gain_row = arrays[0], arrays[5]
    lines, scans = lax.axis_size("line"), lax.axis_size("scan")
    tokens, features = query_row.shape[1:]
    size = gain_row.shape[0]
    heads = features // size
    groups = heads
    arrays = list(arrays)
    arrays[5] = arrays[5].reshape(1, size)
    arrays[10] = arrays[10].reshape(1, size)
    for i in (3, 4):
        arrays[i] = arrays[i].transpose(0, 2, 1)
    for i in (8, 9):
        arrays[i] = arrays[i].transpose(0, 1, 3, 2)
    grouped = (groups, heads // groups, size, size)
    swapped = (groups, lines, heads // groups, tokens // lines, size)
    dma = pltpu.SemaphoreType.DMA
    return pl.pallas_call(
        functools.partial(kernel, lines, scans),
        out_shape=pltpu.VMEM(query_row.shape, BF16),
        in_specs=[pl.BlockSpec(memory_space=pltpu.HBM)] * len(arrays),
        out_specs=pl.BlockSpec(memory_space=pltpu.VMEM),
        scratch_shapes=[pltpu.VMEM(a.shape, a.dtype) for a in arrays]
        + [
            pltpu.VMEM(grouped, BF16),
            pltpu.VMEM((2,) + grouped, BF16),
            pltpu.VMEM((2,) + grouped, BF16),
            pltpu.VMEM(grouped, BF16),
            pltpu.VMEM(grouped, BF16),
            pltpu.VMEM((heads, size, size), F32),
            pltpu.VMEM((heads, tokens, size), F32),
            pltpu.VMEM((heads, tokens, size), BF16),
            pltpu.VMEM((2, heads, tokens, tokens), BF16),
            pltpu.VMEM(swapped, BF16),
            pltpu.VMEM(swapped, BF16),
            pltpu.VMEM(swapped, BF16),
            pltpu.VMEM(swapped, BF16),
            dma((len(arrays),)),
            dma((2, groups)),
            dma((2, groups)),
            dma((2, groups)),
            dma((groups,)),
            dma((groups, lines)),
            dma((groups, lines)),
            dma((groups, lines)),
            dma((groups, lines)),
        ],
        compiler_params=pltpu.CompilerParams(
            collective_id=0, has_side_effects=True, vmem_limit_bytes=60 * 1024 * 1024
        ),
    )(*arrays)


def solution(mesh):
    placed = (
        P("line", "scan", None),
        P("line", "scan", None),
        P("line", "scan", None),
        P("line", "scan", None),
        P("line", "scan", None),
        P(),
        P(None, "scan", "line", None),
        P(None, "scan", "line", None),
        P(None, "scan", "line", None),
        P(None, "scan", "line", None),
        P(),
    )
    return jax.shard_map(
        shards, mesh=mesh, in_specs=placed, out_specs=P("line", "scan", None), check_vma=False
    )
```

```python
import functools

import jax
import jax.numpy as jnp
from jax import lax
from jax.experimental import pallas as pl
from jax.experimental.pallas import tpu as pltpu
from jax.sharding import PartitionSpec as P

F32 = jnp.float32
BF16 = jnp.bfloat16


def dot(a, b):
    return jnp.dot(a, b, preferred_element_type=F32)


def split(a):
    high = a.astype(BF16)
    return high, (a - high.astype(F32)).astype(BF16)


def dot_left(a, b):
    high, low = split(a)
    return dot(high, b) + dot(low, b)


def dot_right(a, b):
    high, low = split(b)
    return dot(a, high) + dot(a, low)


def dot_pairs(a, b):
    return dot(a[0], b[0]) + (dot(a[0], b[1]) + dot(a[1], b[0]))


def masks(size, stride):
    row = lax.broadcasted_iota(jnp.int32, (size, size), 0)
    col = lax.broadcasted_iota(jnp.int32, (size, size), 1)
    same = lax.rem(row, stride) == lax.rem(col, stride)
    return row, col, row == col, same & (row >= col), same & (row > col)


def to_row(column, diagonal):
    return jnp.sum(jnp.where(diagonal, column, 0.0), axis=0, keepdims=True)


def dot16(a, b):
    return dot(a.astype(BF16), b.astype(BF16))


def inverse(systems, row, col, diagonal, stride, steps):
    unit = jnp.where(diagonal, 1.0, 0.0)
    base = min(16, steps)
    near = (row // (base * stride)) == (col // (base * stride))
    power = [jnp.where(near, m, 0.0) for m in systems]
    total = [unit - m for m in power]
    reach = 2
    while reach < base:
        power = [dot16(m, m) for m in power]
        total = [t + dot16(t, m) for t, m in zip(total, power)]
        reach *= 2
    size = base
    while size < steps:
        wide = size * 2 * stride
        link = ((row // wide) == (col // wide)) & (
            (row // (size * stride)) != (col // (size * stride))
        )
        inner = [dot16(jnp.where(link, m, 0.0), t) for m, t in zip(systems, total)]
        total = [t - dot16(t, i) for t, i in zip(total, inner)]
        size *= 2
    return total


def prepare(keys, keys_t, decay, beta, stride):
    size = keys[0].shape[0]
    steps = size // stride
    count = len(keys)
    row, col, diagonal, lower, strict = masks(size, stride)
    rest, cumulative = decay, 0.0
    upper = jnp.where(
        (lax.rem(row, stride) == lax.rem(col, stride)) & (row <= col), 1.0, 0.0
    ).astype(BF16)
    for _ in range(3):
        piece = rest.astype(BF16)
        rest = rest - piece.astype(F32)
        cumulative = cumulative + dot(piece, upper)
    packed = jnp.concatenate([cumulative, beta], axis=0).T
    cum_rows = [cumulative[h : h + 1] for h in range(count)]
    beta_rows = [beta[h : h + 1] for h in range(count)]
    cums = [packed[:, h : h + 1] for h in range(count)]
    systems, ratios, units, unit_rows = [], [], [], []
    for h in range(count):
        gram = dot(keys[h], keys_t[h])
        squares = jnp.where(diagonal, gram, 0.0)
        unit_col = lax.rsqrt(jnp.sum(squares, axis=1, keepdims=True) + 1e-06)
        unit_row = lax.rsqrt(jnp.sum(squares, axis=0, keepdims=True) + 1e-06)
        spread = cums[h] - cum_rows[h]
        ratio = jnp.where(lower, jnp.exp(jnp.where(lower, spread, 0.0)), 0.0) * unit_row
        beta_col = packed[:, count + h : count + h + 1]
        systems.append(jnp.where(strict, (beta_col * unit_col) * (ratio * gram), 0.0))
        ratios.append(ratio)
        units.append(unit_col)
        unit_rows.append(unit_row)
    solved = inverse(systems, row, col, diagonal, stride, steps)
    return solved, ratios, cums, units, cum_rows, beta_rows, unit_rows, diagonal


def normed(block, gain):
    return block * lax.rsqrt(jnp.mean(block * block, axis=-1, keepdims=True) + 1e-05) * gain


def each(count, body):
    if count <= 8:
        for i in range(count):
            body(i)
    else:
        lax.fori_loop(0, count, lambda i, c: (body(i), c)[1], 0)


def kernel(
    lines,
    scans,
    *refs,
):
    hbm, out, held = refs[:11], refs[11], refs[12:23]
    (
        state,
        gift_out,
        gift_in,
        chain_out,
        chain_in,
        offset,
        local,
        asking,
        mixer,
        outgoing,
        incoming,
        returning,
        returned,
        load_sem,
        gift_send,
        gift_recv,
        chain_send,
        chain_recv,
        there_send,
        there_recv,
        back_send,
        back_recv,
    ) = refs[23:]
    (
        query_row,
        key_row,
        value_row,
        decay_row,
        beta_row,
        gain_row,
        query_col,
        key_col,
        decay_col,
        beta_col,
        gain_col,
    ) = held
    me = lax.axis_index("line")
    place = lax.axis_index("scan")
    odd = lax.rem(place, 2)
    tokens, features = query_row.shape[1:]
    size = gain_row.shape[1]
    heads = range(features // size)
    total_rows, width = query_col.shape[0], query_col.shape[2]
    groups = outgoing.shape[0]
    group_heads = outgoing.shape[2]
    mesh_id = pl.DeviceIdType.MESH

    def load(i):
        return pltpu.make_async_copy(hbm[i], held[i], load_sem.at[i])

    for i in (1, 3, 4, 0, 2, 5, 7, 6, 8, 9, 10):
        load(i).start()

    barrier = pltpu.get_barrier_semaphore()

    def greet(i):
        pl.semaphore_signal(
            barrier, inc=1, device_id={"line": lax.rem(me + 1 + i, lines)}, device_id_type=mesh_id
        )

    each(lines - 1, greet)

    def greet_along(distance):
        pl.semaphore_signal(
            barrier, inc=1, device_id={"scan": place + distance}, device_id_type=mesh_id
        )

    pl.when(place > 0)(lambda: greet_along(-1))
    pl.when(place < scans - 1)(lambda: greet_along(1))
    pl.when((odd == 1) & (place > 1))(lambda: greet_along(-2))
    pl.when((odd == 1) & (place < scans - 2))(lambda: greet_along(2))

    def of_head(ref, h):
        return ref[0, :, h * size : (h + 1) * size]

    for i in (1, 3, 4):
        load(i).wait()
    keys = [of_head(key_row, h) for h in heads]
    keys_t = [k.T for k in keys]
    solved, ratios, cums, units, cum_rows, beta_rows, unit_rows, diagonal = prepare(
        keys, keys_t, decay_row[0], beta_row[0], 1
    )
    load(2).wait()
    pl.semaphore_wait(
        barrier,
        lines
        - 1
        + jnp.minimum(place, 1)
        + jnp.minimum(scans - 1 - place, 1)
        + odd * (jnp.minimum(place // 2, 1) + jnp.minimum((scans - 1 - place) // 2, 1)),
    )

    def gift(which, g):
        return pltpu.make_async_remote_copy(
            src_ref=gift_out.at[which, g],
            dst_ref=gift_in.at[which, g],
            send_sem=gift_send.at[which, g],
            recv_sem=gift_recv.at[which, g],
            device_id={"scan": lax.rem(place + 1, scans)},
            device_id_type=mesh_id,
        )

    def chain(g, distance):
        return pltpu.make_async_remote_copy(
            src_ref=chain_out.at[g],
            dst_ref=chain_in.at[g],
            send_sem=chain_send.at[distance - 1, g],
            recv_sem=chain_recv.at[g],
            device_id={"scan": lax.rem(place + distance, scans)},
            device_id_type=mesh_id,
        )

    gives = (odd == 0) & (place < scans - 1)
    lasts = [c[tokens - 1 : tokens, :] for c in cums]
    tails = [jnp.exp(lasts[h] - cums[h]) * units[h] for h in heads]
    updates = [
        dot_left(solved[h] * beta_rows[h], of_head(value_row, h)) for h in heads
    ]
    offsets = [dot(keys_t[h], (tails[h] * updates[h]).astype(BF16)) for h in heads]
    for h in heads:
        gift_out[0, h // group_heads, h % group_heads] = offsets[h].astype(BF16)

    @pl.when(gives)
    def _():
        for g in range(groups):
            gift(0, g).start()

    weighted = {}
    for h in heads:
        offset[h] = offsets[h]
    for h in heads:
        weighted[h] = dot_left(
            solved[h] * (beta_rows[h] * jnp.exp(cum_rows[h]) * unit_rows[h]), keys[h]
        )
        kept = dot(keys_t[h], (tails[h] * weighted[h]).astype(BF16))
        gift_out[1, h // group_heads, h % group_heads] = (
            jnp.where(diagonal, jnp.exp(lasts[h]), 0.0) - kept
        ).astype(BF16)

    @pl.when(gives & (place > 0))
    def _():
        for g in range(groups):
            gift(1, g).start()

    load(0).wait()
    queries = [of_head(query_row, h) for h in heads]
    for h in heads:
        seen = dot_pairs(
            split(ratios[h] * dot(queries[h], keys_t[h])), split(jnp.concatenate([updates[h], weighted[h]], axis=1))
        )
        local[h] = seen[:, :size]
        asking[h] = (
            jnp.exp(cums[h]) * queries[h].astype(F32) - seen[:, size:]
        ).astype(BF16)

    for i in (5, 7, 6, 8, 9, 10):
        load(i).wait()

    def of_head_col(ref, h):
        block = ref[:, 0, :, h * size : (h + 1) * size]
        return block.reshape(total_rows * width, size)

    def column_gates(ref):
        return jnp.concatenate([ref[t, 0] for t in range(total_rows)], axis=1)

    def column_terms():
        col_keys = [of_head_col(key_col, h) for h in heads]
        col_keys_t = [k.T for k in col_keys]
        col_solved, col_ratios, _, _, _, col_betas, _, _ = prepare(
            col_keys, col_keys_t, column_gates(decay_col), column_gates(beta_col), width
        )
        for h in heads:
            attend = col_ratios[h] * dot(of_head_col(query_col, h), col_keys_t[h])
            mixer[0, h], mixer[1, h] = split(
                dot_pairs(split(attend), split(col_solved[h] * col_betas[h]))
            )

    pl.when(place >= 2)(column_terms)

    @pl.when(place == 0)
    def _():
        state[...] = jnp.zeros_like(state)

    def receive_state(g):
        @pl.when(odd == 1)
        def _():
            gift(0, g).wait_recv()

            @pl.when(place == 1)
            def _():
                state[g] = gift_in[0, g]

            @pl.when(place > 1)
            def _():
                gift(1, g).wait_recv()
                chain(g, 1).wait_recv()
                for j in range(group_heads):
                    state[g, j] = (
                        dot(gift_in[1, g, j], chain_in[g, j]) + gift_in[0, g, j].astype(F32)
                    ).astype(BF16)

            @pl.when(place < scans - 1)
            def _():
                for j in range(group_heads):
                    chain_out[g, j] = (
                        dot(gift_out[1, g, j], state[g, j]) + offset[g * group_heads + j]
                    ).astype(BF16)
                chain(g, 1).start()
                pl.when(place < scans - 2)(lambda: chain(g, 2).start())

        @pl.when((odd == 0) & (place > 0))
        def _():
            chain(g, 1).wait_recv()
            state[g] = chain_in[g]

    def swap(source, target, send, recv, g, i):
        peer = lax.rem(me + 1 + i, lines)
        return pltpu.make_async_remote_copy(
            src_ref=source.at[g, peer],
            dst_ref=target.at[g, me],
            send_sem=send.at[g, i],
            recv_sem=recv.at[g, me],
            device_id={"line": peer},
            device_id_type=mesh_id,
        )

    def receive(source, target, send, recv, g, i):
        peer = lax.rem(me + 1 + i, lines)
        pltpu.make_async_remote_copy(
            src_ref=source.at[g, peer],
            dst_ref=target.at[g, peer],
            send_sem=send.at[g, i],
            recv_sem=recv.at[g, peer],
            device_id={"line": peer},
            device_id_type=mesh_id,
        ).wait_recv()

    there = (outgoing, incoming, there_send, there_recv)
    back = (returning, returned, back_send, back_recv)

    forwards = (odd == 1) & (place < scans - 1)

    @pl.when(forwards)
    def _():
        for g in range(groups):
            receive_state(g)

    for g in range(groups):
        pl.when(jnp.logical_not(forwards))(functools.partial(receive_state, g))
        for j in range(group_heads):
            h = g * group_heads + j
            row_out = local[h] + dot(asking[h], state[g, j])
            values = normed(row_out, gain_row[...]).astype(BF16)
            outgoing[g, :, j] = values.reshape(lines, tokens // lines, size)
        each(lines - 1, lambda i: swap(*there, g, i).start())
        incoming[g, me] = outgoing[g, me]

    pl.when(place < 2)(column_terms)

    for g in range(groups):
        each(lines - 1, lambda i: receive(*there, g, i))
        for j in range(group_heads):
            h = g * group_heads + j
            values = incoming[g, :, j].reshape(total_rows * width, size)
            mixed = normed(
                dot(mixer[0, h], values) + dot(mixer[1, h], values), gain_col[...]
            ).astype(BF16)
            returning[g, :, j] = mixed.reshape(total_rows, width, size)
        each(lines - 1, lambda i: swap(*back, g, i).start())
        returned[g, me] = returning[g, me]

    for g in range(groups):
        each(lines - 1, lambda i: receive(*back, g, i))
        for j in range(group_heads):
            h = g * group_heads + j
            out[0, :, h * size : (h + 1) * size] = returned[g, :, j].reshape(tokens, size)

    for g in range(groups):
        each(lines - 1, lambda i: swap(*there, g, i).wait_send())
        each(lines - 1, lambda i: swap(*back, g, i).wait_send())

    @pl.when(gives)
    def _():
        for g in range(groups):
            gift(0, g).wait_send()
            pl.when(place > 0)(lambda: gift(1, g).wait_send())

    @pl.when((odd == 1) & (place < scans - 1))
    def _():
        for g in range(groups):
            chain(g, 1).wait_send()
            pl.when(place < scans - 2)(lambda: chain(g, 2).wait_send())


def shards(*arrays):
    query_row, gain_row = arrays[0], arrays[5]
    lines, scans = lax.axis_size("line"), lax.axis_size("scan")
    tokens, features = query_row.shape[1:]
    size = gain_row.shape[0]
    heads = features // size
    groups = heads
    arrays = list(arrays)
    arrays[5] = arrays[5].reshape(1, size)
    arrays[10] = arrays[10].reshape(1, size)
    for i in (3, 4):
        arrays[i] = arrays[i].transpose(0, 2, 1)
    for i in (8, 9):
        arrays[i] = arrays[i].transpose(0, 1, 3, 2)
    grouped = (groups, heads // groups, size, size)
    swapped = (groups, lines, heads // groups, tokens // lines, size)
    dma = pltpu.SemaphoreType.DMA
    return pl.pallas_call(
        functools.partial(kernel, lines, scans),
        out_shape=pltpu.VMEM(query_row.shape, BF16),
        in_specs=[pl.BlockSpec(memory_space=pltpu.HBM)] * len(arrays),
        out_specs=pl.BlockSpec(memory_space=pltpu.VMEM),
        scratch_shapes=[pltpu.VMEM(a.shape, a.dtype) for a in arrays]
        + [
            pltpu.VMEM(grouped, BF16),
            pltpu.VMEM((2,) + grouped, BF16),
            pltpu.VMEM((2,) + grouped, BF16),
            pltpu.VMEM(grouped, BF16),
            pltpu.VMEM(grouped, BF16),
            pltpu.VMEM((heads, size, size), F32),
            pltpu.VMEM((heads, tokens, size), F32),
            pltpu.VMEM((heads, tokens, size), BF16),
            pltpu.VMEM((2, heads, tokens, tokens), BF16),
            pltpu.VMEM(swapped, BF16),
            pltpu.VMEM(swapped, BF16),
            pltpu.VMEM(swapped, BF16),
            pltpu.VMEM(swapped, BF16),
            dma((len(arrays),)),
            dma((2, groups)),
            dma((2, groups)),
            dma((2, groups)),
            dma((groups,)),
            dma((groups, lines)),
            dma((groups, lines)),
            dma((groups, lines)),
            dma((groups, lines)),
        ],
        compiler_params=pltpu.CompilerParams(
            collective_id=0, has_side_effects=True, vmem_limit_bytes=60 * 1024 * 1024
        ),
    )(*arrays)


def solution(mesh):
    placed = (
        P("line", "scan", None),
        P("line", "scan", None),
        P("line", "scan", None),
        P("line", "scan", None),
        P("line", "scan", None),
        P(),
        P(None, "scan", "line", None),
        P(None, "scan", "line", None),
        P(None, "scan", "line", None),
        P(None, "scan", "line", None),
        P(),
    )
    return jax.shard_map(
        shards, mesh=mesh, in_specs=placed, out_specs=P("line", "scan", None), check_vma=False
    )
```
